128 devices in a mesh: wide: 16 (over z, x), narrow: 8 (over y, core).
Axes of the slice: x: 4, y: 4, z: 4, core: 2. Of those that a mesh axis runs over, the one named last changes fastest.
Arguments:
- scalars: float32 [16384, 16, 128], P(('wide', 'narrow')), may hold values from -6 to 6
- mass: float32 [16384, 128], P(('wide', 'narrow')), may hold values from 0.2 to 5
- frequency: float32 [16384, 128], P(('wide', 'narrow')), may hold values from 0.02 to 4
- cell: int32 [16384, 128], P(('wide', 'narrow')), may hold values from 0 to 1299
- owner: int32 [16384, 1], P(('wide', 'narrow')), may hold values from 0 to 127; in each aligned block of 128 rows (0 to 127, 128 to 255, ...) at most 2 rows name the same one
Outputs:
- mixed: float32 [16384, 16, 128], P(('wide', 'narrow'))
- cell_mean: float32 [16, 128, 1024], P(None, 'wide', 'narrow')
The draws below stay inside these ranges and needn't reach their ends.
Inputs may be any that keep to these rules, and one draw needn't show every extreme that they name: The blocks of one device name any one owner at most 2 times, a bound that some block reaches.
All inputs are finite; a program needn't handle non-finite values.
Results may differ from the reference program's by a relative error of at most 0.000084.
Values sent between devices are 32-bit elements; how exact they have to be, the bound alone decides.
A program may use at most 64 MiB of HBM per device.

```python
import math
import jax
import jax.numpy as jnp
import numpy as np

S = 16
BP = 128
NB = 128
CW = 8
CN = 128
CAP = 2
EXT = 1300
NBT = 16384
NX = 128
NY = 1024
N_NARROW = 8
DEVICES = 128


def with_ends(values, own_key, least, top_value):
    dims = values.shape
    place = [jax.random.randint(jax.random.fold_in(own_key, axis), (), 0, dims[axis]) for axis in range(len(dims))]
    values = values.at[tuple(place)].set(least)
    longest = dims.index(max(dims))
    place[longest] = (place[longest] + 1) % dims[longest]
    return values.at[tuple(place)].set(top_value)


def block_levels(key, extent, split, least, high):
    loudness = 1.0
    for axis_at, parts in split:
        draws = jax.random.uniform(jax.random.fold_in(jax.random.fold_in(key, 6), axis_at), (parts,), jnp.float32, least / len(split), high / len(split))
        loudness = loudness * jnp.repeat(jnp.exp(draws), extent[axis_at] // parts).reshape((-1,) + (1,) * (len(extent) - 1 - axis_at))
    return loudness


def routed_block(rng, own, number, rows, amount, top, most, lean):
    order = jax.random.permutation(rng, amount)
    packed, usual = load_shares(amount, rows * top, most, lean, True), load_shares(amount, rows * top, most, lean, False)
    places = jnp.arange(amount)

    def named(lengths, rotation):
        used = int((lengths > 0).sum())
        fixed = max(1, used // 4)
        shifted = fixed + (places - fixed + rotation * (used - fixed)) % max(1, amount - fixed)
        return jnp.zeros((amount,), jnp.int32).at[order[jnp.where(places < fixed, places, shifted)]].set(jnp.asarray(lengths, jnp.int32))

    lengths = jnp.where(number % 4 == 0, named(packed, number // 4), named(usual, number - number // 4 - 1))
    mixed = jax.random.permutation(jax.random.fold_in(own, 3), amount)
    source_of, sink = mixed[0:amount // 2 * 2:2], mixed[1:amount // 2 * 2:2]
    slack = jnp.minimum(lengths[source_of] - 1, most - lengths[sink]) // 2
    slack = jnp.where((source_of == order[0]) | (sink == order[0]) | (lengths[sink] == 0), 0, jnp.maximum(slack, 0))
    shifted = jax.random.randint(jax.random.fold_in(own, 4), (amount // 2,), 0, 1 << 20) % (slack + 1)
    lengths = lengths.at[source_of].add(-shifted).at[sink].add(shifted)
    items = jnp.searchsorted(jnp.cumsum(lengths), jnp.arange(rows * top), side="right").astype(jnp.int32)
    listing = items.reshape(top, rows).T
    listing = listing[jax.random.permutation(jax.random.fold_in(own, 1), rows)]
    rotation = jax.random.randint(jax.random.fold_in(own, 2), (rows, 1), 0, top)
    return jnp.take_along_axis(listing, (jnp.arange(top)[None, :] + rotation) % top, axis=1)


def load_shares(number_of, total, limit, skew, full):
    weights = [(1 << 20) // math.isqrt(grade ** skew) + 1 for grade in range(1, number_of + 1)]
    largest = limit if full else min(limit, max(-(-total // number_of), total * weights[0] // sum(weights)))
    least = 1 if total - largest >= number_of - 1 else 0
    counts, surplus = [largest] + [least] * (number_of - 1), total - largest - least * (number_of - 1)
    while surplus > 0:
        candidates = [i for i in range(1, number_of) if counts[i] < largest] or [i for i in range(1, number_of) if counts[i] < limit]
        pool, left = sum([weights[i] for i in candidates]), surplus
        for i in candidates:
            extra = min(limit - counts[i], max(1, left * weights[i] // pool), surplus)
            counts[i] = counts[i] + extra
            surplus = surplus - extra
    return np.array(counts)


def bell_draw(own_key, dims, width, limit, pieces=(), kind=jnp.bfloat16):
    result = width * jax.random.normal(own_key, dims, jnp.float32)
    if pieces:
        result = result * block_levels(own_key, dims, pieces, -0.22, 0.18)
    return jnp.clip(result, -limit, limit).astype(kind)


def setup_inputs(seed: int = 0) -> dict:
    key_list = jax.random.split(jax.random.key(seed), 6)
    scalars = bell_draw(key_list[0], (NBT, S, BP), 1.0, 6.0, ((0, 128),), jnp.float32)
    mass = jnp.clip(jnp.exp(math.log(5.0) - 3.218876 * jax.random.uniform(key_list[1], (NBT, BP), jnp.float32) ** block_levels(key_list[1], (NBT, BP), ((0, 128),), -0.2, 0.2)), 0.2, 5.0)
    frequency = jnp.clip(jnp.exp(math.log(4.0) - 5.2983174 * jax.random.uniform(key_list[2], (NBT, BP), jnp.float32) ** block_levels(key_list[2], (NBT, BP), ((0, 128),), -0.2, 0.2)), 0.02, 4.0)
    cell = with_ends(jax.random.randint(key_list[3], (NBT, BP), 0, EXT), jax.random.fold_in(key_list[3], 1), 0, EXT - 1).astype(jnp.int32)
    owner_keys = jax.random.split(jax.random.fold_in(key_list[4], 1), NBT // NB)
    owner_turns = jax.random.permutation(jax.random.fold_in(key_list[4], 3), NBT // NB)
    owner = jax.vmap(lambda own, number: routed_block(jax.random.fold_in(key_list[4], 2), own, number, NB, DEVICES, 1, CAP, 2))(owner_keys, owner_turns).reshape((NBT, 1))
    return dict(scalars=scalars, mass=mass, frequency=frequency, cell=cell, owner=owner)


def reference(scalars, mass, frequency, cell, owner):
    block_total = scalars.shape[0]
    target = owner[:, 0]
    wide_pos = target // N_NARROW
    narrow_pos = target % N_NARROW
    cycle_row = cell // (CN + 2)
    cycle_col = cell % (CN + 2)
    grid_row = (wide_pos[:, None] * CW + cycle_row - 1) % NX
    grid_col = (narrow_pos[:, None] * CN + cycle_col - 1) % NY
    grid_cell = (grid_row * NY + grid_col).reshape(-1).astype(jnp.int32)
    weighted = scalars * mass[:, None, :]
    columns = jnp.concatenate([jnp.transpose(weighted, (0, 2, 1)).reshape(-1, S), mass.reshape(-1, 1)], axis=1)
    sums = jax.ops.segment_sum(columns, grid_cell, num_segments=NX * NY)
    means = sums[:, :S] / (sums[:, S:] + 1.0)
    near = jnp.take(means, grid_cell, axis=0).reshape(block_total, BP, S)
    near = jnp.transpose(near, (0, 2, 1))
    rate = frequency * (1.5 + jnp.tanh(near[:, 0, :]))
    mixed = near + (scalars - near) * jnp.exp(-rate)[:, None, :]
    cell_mean = means.T.reshape(S, NX, NY)
    return mixed, cell_mean
```

```python
import functools

import jax
import jax.numpy as jnp
from jax import lax
from jax.experimental import pallas as pl
from jax.experimental.pallas import tpu as pltpu
from jax.sharding import PartitionSpec as P

CW = 8
CN = 128
ROWS = CW + 2
COLS = CN + 2
MESH = pl.DeviceIdType.MESH
GROUP = 4


def kernel(
    devices,
    scal_ref,
    mass_ref,
    freq_ref,
    cell_ref,
    owner_ref,
    mixed_ref,
    mean_ref,
    out_buf,
    got_buf,
    near_buf,
    ret_buf,
    left_buf,
    hot_buf,
    acc_ref,
    tile_ref,
    side_buf,
    up_buf,
    side_got,
    diag_got,
    mean_buf,
    idx_vm,
    idx_sm,
    row_buf,
    weight_ref,
    idx_sem,
    send_sem,
    recv_sem,
    back_send,
    back_recv,
    halo_send,
    halo_recv,
):
    f32, bf16 = jnp.float32, jnp.bfloat16
    wide = lax.axis_index("wide")
    narrow = lax.axis_index("narrow")
    me = wide * 8 + narrow
    z, x, y, c = wide // 4, wide % 4, narrow // 2, narrow % 2

    def offsets(k):
        a, b, d, e = k % 4, (k // 4) % 4, (k // 16) % 4, k // 64
        return a, (a + b) % 4, (d + 4 - a) % 4, e

    def ahead(k):
        dz, dx, dy, dc = offsets(k)
        return ((z + dz) % 4) * 4 + (x + dx) % 4, ((y + dy) % 4) * 2 + (c + dc) % 2

    def behind(k):
        dz, dx, dy, dc = offsets(k)
        return (
            ((z + 4 - dz) % 4) * 4 + (x + 4 - dx) % 4,
            ((y + 4 - dy) % 4) * 2 + (c + 2 - dc) % 2,
        )

    lanes = owner_ref.shape[1]
    along = jnp.broadcast_to(owner_ref[...], (lanes, lanes))
    down = along.T
    sub = lax.broadcasted_iota(jnp.int32, (lanes, lanes), 0)
    lane = lax.broadcasted_iota(jnp.int32, (lanes, lanes), 1)
    match = down == lane
    first = jnp.min(jnp.where(match, sub, lanes), axis=0, keepdims=True)
    second = jnp.max(jnp.where(match, sub, -1), axis=0, keepdims=True)
    earlier = jnp.where((down == along) & (sub < lane), 1, 0)
    place = 2 * owner_ref[...] + jnp.max(earlier, axis=0, keepdims=True)
    idx_vm[0:1, :] = jnp.minimum(first, lanes - 1)
    idx_vm[1:2, :] = jnp.maximum(second, 0)
    idx_vm[2:3, :] = first
    idx_vm[3:4, :] = jnp.where(second > first, second, lanes)
    idx_vm[4:5, :] = place
    idx_vm[5:8, :] = jnp.zeros((3, lanes), jnp.int32)
    to_scalar = pltpu.make_async_copy(idx_vm, idx_sm, idx_sem)
    to_scalar.start()
    weight_ref[0:lanes, :] = mass_ref[...]
    weight_ref[lanes : lanes + 8, :] = jnp.zeros((8, CN), f32)
    acc_ref[...] = jnp.zeros_like(acc_ref)
    hot_buf[...] = jnp.zeros_like(hot_buf)
    to_scalar.wait()

    def pack(dest, owner):
        for slot in range(2):
            b = idx_sm[slot, owner]
            m = weight_ref[pl.ds(idx_sm[2 + slot, owner], 1), :]
            dest[16 * slot : 16 * slot + 16, :] = scal_ref[b] * m
            dest[32 + slot : 33 + slot, :] = m
            dest[34 + slot : 35 + slot, :] = cell_ref[pl.ds(b, 1), :].astype(f32)

    def send(k):
        w, v = ahead(k)
        return pltpu.make_async_remote_copy(
            out_buf.at[k],
            got_buf.at[k],
            send_sem,
            recv_sem.at[k],
            device_id=(w, v),
            device_id_type=MESH,
        )

    def send_step(k, carry):
        w, v = ahead(k)
        pack(out_buf.at[k], w * 8 + v)
        send(k).start()
        return carry

    lax.fori_loop(1, devices, send_step, 0)
    pack(got_buf.at[0], me)

    tile_row = lax.broadcasted_iota(jnp.int32, (16, CN), 0).astype(f32)

    def place_of(cells):
        i = jnp.floor((cells + 0.5) * (1.0 / COLS))
        j = cells - i * COLS - 1.0
        return i, jnp.where(j < 0.0, COLS - 1.0, j)

    def fill_hot(j, lane_at):
        j16 = jnp.broadcast_to(j, (16, CN)).astype(bf16)
        for t in range(-(-COLS // 16)):
            hot_buf[16 * t : 16 * t + 16, lane_at : lane_at + CN] = jnp.where(
                (tile_row + 16.0 * t).astype(bf16) == j16, 1.0, 0.0
            ).astype(bf16)

    def deposit(g):
        for n in range(GROUP):
            for slot in range(2):
                at = (2 * n + slot) * CN
                k = g * GROUP + n
                value = got_buf[k, 16 * slot : 16 * slot + 16, :]
                m = got_buf[k, 32 + slot : 33 + slot, :]
                i, j = place_of(got_buf[k, 34 + slot : 35 + slot, :])
                fill_hot(j, at)
                hi = value.astype(bf16)
                lo = (value - hi.astype(f32)).astype(bf16)
                i16 = jnp.broadcast_to(i, (16, CN)).astype(bf16)
                none = jnp.zeros((16, CN), bf16)
                for r in range(ROWS):
                    mask = i16 == jnp.full((16, CN), r, bf16)
                    left_buf[16 * r : 16 * r + 16, at : at + CN] = jnp.where(mask, hi, none)
                    left_buf[160 + 16 * r : 176 + 16 * r, at : at + CN] = jnp.where(mask, lo, none)
                m16 = jnp.broadcast_to(m, (16, CN))
                mhi = m16.astype(bf16)
                mlo = (m16 - mhi.astype(f32)).astype(bf16)
                mask = i16 == tile_row.astype(bf16)
                left_buf[320:336, at : at + CN] = jnp.where(mask, mhi, none)
                left_buf[336:352, at : at + CN] = jnp.where(mask, mlo, none)
        acc_ref[...] += lax.dot_general(
            left_buf[...],
            hot_buf[...],
            (((1,), (1,)), ((), ())),
            preferred_element_type=f32,
        )

    for n in range(1, GROUP):
        send(n).wait_recv()
    deposit(0)

    def deposit_step(g, carry):
        for n in range(GROUP):
            send(g * GROUP + n).wait_recv()
        deposit(g)
        return carry

    lax.fori_loop(1, devices // GROUP, deposit_step, 0)

    tile_ref[0:8, :] = acc_ref[320:328, :] + acc_ref[336:344, :]
    tile_ref[8:168, :] = acc_ref[0:160, :] + acc_ref[160:320, :]
    tile_ref[168:176, :] = acc_ref[328:336, :] + acc_ref[344:352, :]
    own, rest = tile_ref[:, 0:128], tile_ref[:, 128:256]
    at_lane = lax.broadcasted_iota(jnp.int32, (176, 128), 1)
    side_buf[0] = jnp.where(at_lane == 127, pltpu.roll(rest, 126, 1), own)
    side_buf[1] = jnp.where(at_lane == 0, rest, pltpu.roll(own, 2, 1))
    above, below = (wide + 15) % 16, (wide + 1) % 16
    before, after = (narrow + 7) % 8, (narrow + 1) % 8
    top, bottom = pl.ds(0, 40), pl.ds(136, 40)
    halo = [
        (tile_ref.at[top], up_buf.at[1], (above, narrow)),
        (tile_ref.at[bottom], up_buf.at[0], (below, narrow)),
        (side_buf.at[0], side_got.at[1], (wide, before)),
        (side_buf.at[1], side_got.at[0], (wide, after)),
        (side_buf.at[0, top], diag_got.at[3], (above, before)),
        (side_buf.at[0, bottom], diag_got.at[1], (below, before)),
        (side_buf.at[1, top], diag_got.at[2], (above, after)),
        (side_buf.at[1, bottom], diag_got.at[0], (below, after)),
    ]
    halo = [
        pltpu.make_async_remote_copy(
            src, dst, halo_send.at[n], halo_recv.at[n], device_id=to, device_id_type=MESH
        )
        for n, (src, dst, to) in enumerate(halo)
    ]
    for copy in halo:
        copy.start()
    for copy in halo:
        copy.wait()
    nothing = jnp.zeros((96, 128), f32)

    def with_corners(side, high, low):
        return side + jnp.concatenate(
            [high[32:40], high[0:32], nothing, low[8:40], low[0:8]], axis=0
        )

    from_left = with_corners(side_got[0], diag_got[0], diag_got[2])
    from_right = with_corners(side_got[1], diag_got[1], diag_got[3])
    high, low = up_buf[0], up_buf[1]
    nothing2 = jnp.zeros((96, 256), f32)
    vertical = jnp.concatenate(
        [high[32:40], high[0:32], nothing2, low[8:40], low[0:8]], axis=0
    )
    own = (
        own
        + vertical[:, 0:128]
        + jnp.where(at_lane == 0, from_left, 0.0)
        + jnp.where(at_lane == 127, from_right, 0.0)
    )
    rest = (
        rest
        + vertical[:, 128:256]
        + jnp.where(at_lane == 1, from_left, 0.0)
        + jnp.where(at_lane == 0, from_right, 0.0)
    )
    total = jnp.concatenate([own, rest], axis=1)
    for r in range(ROWS):
        at = r if r < 8 else 160 + r
        mean = total[8 + 16 * r : 24 + 16 * r, :] / (total[at : at + 1, :] + 1.0)
        if 1 <= r <= CW:
            mean_ref[:, r - 1, :] = mean[:, 0:CN]
        hi = mean.astype(bf16)
        mean_buf[16 * r : 16 * r + 16, :] = hi
        mean_buf[160 + 16 * r : 176 + 16 * r, :] = (mean - hi.astype(f32)).astype(bf16)

    def lookup(g):
        rows = []
        for n in range(GROUP):
            for slot in range(2):
                k = g * GROUP + n
                i, j = place_of(got_buf[k, 34 + slot : 35 + slot, :])
                fill_hot(j, (2 * n + slot) * CN)
                rows.append(i)
        for n in range(GROUP):
            k = g * GROUP + n
            found = jnp.dot(
                mean_buf[...],
                hot_buf[:, 256 * n : 256 * n + 256],
                preferred_element_type=f32,
            )
            for slot in range(2):
                i16 = jnp.broadcast_to(rows[2 * n + slot], (16, CN))
                near = jnp.zeros((16, CN), f32)
                cut = slice(CN * slot, CN * slot + CN)
                for r in range(ROWS):
                    near = near + jnp.where(
                        i16 == float(r),
                        found[16 * r : 16 * r + 16, cut] + found[160 + 16 * r : 176 + 16 * r, cut],
                        0.0,
                    )
                near_buf[2 * k + slot] = near

    def give_back(k):
        w, v = behind(k)
        return pltpu.make_async_remote_copy(
            near_buf.at[pl.ds(2 * k, 2)],
            ret_buf.at[pl.ds(2 * me, 2)],
            back_send,
            back_recv.at[k],
            device_id=(w, v),
            device_id_type=MESH,
        )

    def take_back(k):
        w, v = ahead(k)
        return pltpu.make_async_remote_copy(
            near_buf.at[pl.ds(2 * k, 2)],
            ret_buf.at[pl.ds(2 * (w * 8 + v), 2)],
            back_send,
            back_recv.at[k],
            device_id=(w, v),
            device_id_type=MESH,
        )

    lookup(0)
    ret_buf[pl.ds(2 * me, 2)] = near_buf[0:2]
    for n in range(1, GROUP):
        give_back(n).start()

    def lookup_step(g, carry):
        lookup(g)
        for n in range(GROUP):
            give_back(g * GROUP + n).start()
        return carry

    lax.fori_loop(1, devices // GROUP, lookup_step, 0)

    def arrive(k, carry):
        take_back(k).wait_recv()
        return carry

    lax.fori_loop(1, devices, arrive, 0)

    def read_rate(b, carry):
        p = idx_sm[4, b]
        row_buf[pl.ds(b, 1), :] = ret_buf[p, 0:1, :]
        return carry

    lax.fori_loop(0, lanes, read_rate, 0, unroll=4)
    row_buf[...] = jnp.exp(-freq_ref[...] * (1.5 + jnp.tanh(row_buf[...])))

    def mix(b, carry):
        p = idx_sm[4, b]
        near = ret_buf[p]
        mixed_ref[b] = near + (scal_ref[b] - near) * row_buf[pl.ds(b, 1), :]
        return carry

    lax.fori_loop(0, lanes, mix, 0, unroll=4)

    rest_of = pl.ds(1, devices - 1)
    pltpu.make_async_copy(out_buf.at[rest_of], got_buf.at[rest_of], send_sem).wait()
    rest_of = pl.ds(2, 2 * (devices - 1))
    pltpu.make_async_copy(near_buf.at[rest_of], ret_buf.at[rest_of], back_send).wait()


def per_device(scalars, mass, frequency, cell, owner):
    devices = lax.axis_size("wide") * lax.axis_size("narrow")
    blocks, count, per_block = scalars.shape
    f32, bf16 = jnp.float32, jnp.bfloat16
    vmem = pl.BlockSpec(memory_space=pltpu.VMEM)
    return pl.pallas_call(
        functools.partial(kernel, devices),
        out_shape=(
            jax.ShapeDtypeStruct((blocks, count, per_block), f32),
            jax.ShapeDtypeStruct((count, CW, CN), f32),
        ),
        in_specs=[vmem] * 5,
        out_specs=(vmem, vmem),
        scratch_shapes=[
            pltpu.VMEM((devices, 36, per_block), f32),
            pltpu.VMEM((devices, 36, per_block), f32),
            pltpu.VMEM((2 * devices, 16, per_block), f32),
            pltpu.VMEM((2 * devices, 16, per_block), f32),
            pltpu.VMEM((352, GROUP * 256), bf16),
            pltpu.VMEM((256, GROUP * 256), bf16),
            pltpu.VMEM((352, 256), f32),
            pltpu.VMEM((176, 256), f32),
            pltpu.VMEM((2, 176, 128), f32),
            pltpu.VMEM((2, 40, 256), f32),
            pltpu.VMEM((2, 176, 128), f32),
            pltpu.VMEM((4, 40, 128), f32),
            pltpu.VMEM((320, 256), bf16),
            pltpu.VMEM((8, blocks), jnp.int32),
            pltpu.SMEM((8, blocks), jnp.int32),
            pltpu.VMEM((blocks, per_block), f32),
            pltpu.VMEM((blocks + 8, per_block), f32),
            pltpu.SemaphoreType.DMA,
            pltpu.SemaphoreType.DMA,
            pltpu.SemaphoreType.DMA((devices,)),
            pltpu.SemaphoreType.DMA,
            pltpu.SemaphoreType.DMA((devices,)),
            pltpu.SemaphoreType.DMA((8,)),
            pltpu.SemaphoreType.DMA((8,)),
        ],
        compiler_params=pltpu.CompilerParams(
            has_side_effects=True, vmem_limit_bytes=48 << 20
        ),
        name="mixing",
    )(scalars, mass, frequency, cell, owner.reshape(1, blocks))


def solution(mesh):
    held = P(("wide", "narrow"), None)
    block = P(("wide", "narrow"), None, None)
    return jax.shard_map(
        per_device,
        mesh=mesh,
        in_specs=(block, held, held, held, held),
        out_specs=(block, P(None, "wide", "narrow")),
        check_vma=False,
    )
```

```python
import functools

import jax
import jax.numpy as jnp
from jax import lax
from jax.experimental import pallas as pl
from jax.experimental.pallas import tpu as pltpu
from jax.sharding import PartitionSpec as P

CW = 8
CN = 128
ROWS = CW + 2
COLS = CN + 2
MESH = pl.DeviceIdType.MESH
GROUP = 4


def kernel(
    devices,
    scal_hbm,
    mass_hbm,
    freq_hbm,
    cell_hbm,
    owner_hbm,
    mixed_ref,
    mean_ref,
    out_buf,
    got_buf,
    near_buf,
    ret_buf,
    scal_ref,
    freq_ref,
    cell_ref,
    owner_ref,
    left_even,
    left_odd,
    hot_even,
    hot_odd,
    acc_ref,
    tile_ref,
    side_buf,
    up_buf,
    side_got,
    diag_got,
    mean_buf,
    idx_vm,
    idx_sm,
    row_buf,
    weight_ref,
    load_sem,
    hello_sem,
    idx_sem,
    send_sem,
    recv_sem,
    back_send,
    back_recv,
    halo_send,
    halo_recv,
):
    f32, bf16 = jnp.float32, jnp.bfloat16
    left_bufs, hot_bufs = (left_even, left_odd), (hot_even, hot_odd)
    wide = lax.axis_index("wide")
    narrow = lax.axis_index("narrow")
    me = wide * 8 + narrow
    here = (lax.div(wide, 4), lax.rem(wide, 4), lax.div(narrow, 2), lax.rem(narrow, 2))

    def at_offset(offset, sign=1):
        z, x, y, c = (
            lax.rem(h + (d if sign > 0 else n - d), n) for h, d, n in zip(here, offset, (4, 4, 4, 2))
        )
        return z * 4 + x, y * 2 + c

    near_by = [(0, 0, 0, 1)]
    for d in (1, 3, 2):
        near_by += [(d, 0, 0, 0), (0, d, 0, 0), (0, 0, d, 0)]

    def two_axes(i):
        a, b = 1 + lax.div(i, 3), 1 + lax.rem(i, 3)
        on = [1 - lax.div(lax.rem(b - 1 + n, 3) + 1, 2) for n in (0, 2, 1)]
        return [(a, b, 0, 0), (b, 0, a, 0), (0, a, b, 0), (on[0] * a, on[1] * a, on[2] * a, 1)]

    def three_axes(i):
        a, b = 1 + lax.div(i, 3), 1 + lax.rem(i, 3)
        last = [(a, b, n, 0) for n in (1, 2, 3)]
        return [last[0], (a, b, 0, 1), last[1], (b, 0, a, 1), last[2], (0, a, b, 1)]

    def four_axes(i):
        a, b = 1 + lax.div(i, 3), 1 + lax.rem(i, 3)
        return [(a, b, n, 1) for n in (1, 2, 3)]

    classes = [(11, 9, two_axes), (47, 9, three_axes), (101, 9, four_axes)]

    def hello(sem):
        for offset in near_by:
            pl.semaphore_signal(sem, inc=1, device_id=at_offset(offset), device_id_type=MESH)

    barrier = pltpu.get_barrier_semaphore()
    hello(barrier)
    loads = [
        pltpu.make_async_copy(src, dst, load_sem.at[n])
        for n, (src, dst) in enumerate(
            (
                (owner_hbm, owner_ref),
                (scal_hbm, scal_ref),
                (mass_hbm, weight_ref.at[pl.ds(0, mass_hbm.shape[0])]),
                (cell_hbm, cell_ref),
                (freq_hbm, freq_ref),
            )
        )
    ]
    for copy in loads:
        copy.start()

    lanes = owner_ref.shape[1]
    weight_ref[lanes : lanes + 8, :] = jnp.zeros((8, CN), f32)
    acc_ref[...] = jnp.zeros_like(acc_ref)
    for hot_buf in hot_bufs:
        hot_buf[144:256, :] = jnp.zeros((112, hot_buf.shape[1]), bf16)
    loads[0].wait()
    along = jnp.broadcast_to(owner_ref[...], (lanes, lanes))
    down = along.T
    sub = lax.broadcasted_iota(jnp.int32, (lanes, lanes), 0)
    lane = lax.broadcasted_iota(jnp.int32, (lanes, lanes), 1)
    match = down == lane
    first = jnp.min(jnp.where(match, sub, lanes), axis=0, keepdims=True)
    second = jnp.max(jnp.where(match, sub, -1), axis=0, keepdims=True)
    earlier = jnp.where((down == along) & (sub < lane), 1, 0)
    place = 2 * owner_ref[...] + jnp.max(earlier, axis=0, keepdims=True)
    idx_vm[0:1, :] = jnp.minimum(first, lanes - 1)
    idx_vm[1:2, :] = jnp.maximum(second, 0)
    idx_vm[2:3, :] = first
    idx_vm[3:4, :] = jnp.where(second > first, second, lanes)
    idx_vm[4:5, :] = place
    idx_vm[5:8, :] = jnp.zeros((3, lanes), jnp.int32)
    to_scalar = pltpu.make_async_copy(idx_vm, idx_sm, idx_sem)
    to_scalar.start()
    to_scalar.wait()
    for copy in loads[1:]:
        copy.wait()

    def pack(dest, owner):
        for slot in range(2):
            b = idx_sm[slot, owner]
            m = weight_ref[pl.ds(idx_sm[2 + slot, owner], 1), :]
            dest[16 * slot : 16 * slot + 16, :] = scal_ref[b] * m
            dest[32 + slot : 33 + slot, :] = m
            dest[34 + slot : 35 + slot, :] = cell_ref[pl.ds(b, 1), :].astype(f32)

    def send_to(p, offset):
        w, v = at_offset(offset)
        pack(out_buf.at[p], w * 8 + v)
        pltpu.make_async_remote_copy(
            out_buf.at[p],
            got_buf.at[p],
            send_sem,
            recv_sem.at[p],
            device_id=(w, v),
            device_id_type=MESH,
        ).start()

    def send_class(base, steps, offsets):
        def body(i, carry):
            listed = offsets(i)
            for n, offset in enumerate(listed):
                send_to(base + len(listed) * i + n, offset)
            return carry

        lax.fori_loop(0, steps, body, 0)

    pl.semaphore_wait(barrier, len(near_by))
    hello(hello_sem.at[0])
    for n, offset in enumerate(near_by):
        send_to(1 + n, offset)
    pl.semaphore_wait(hello_sem.at[0], len(near_by))
    hello(hello_sem.at[1])
    send_class(*classes[0])
    pl.semaphore_wait(hello_sem.at[1], len(near_by))
    hello(hello_sem.at[2])
    send_class(*classes[1])
    pl.semaphore_wait(hello_sem.at[2], len(near_by))
    send_class(*classes[2])
    pack(got_buf.at[0], me)

    tile_row = lax.broadcasted_iota(jnp.int32, (16, CN), 0).astype(f32)
    row16 = tile_row.astype(bf16)
    none, one = jnp.zeros((16, CN), bf16), jnp.ones((16, CN), bf16)

    def place_of(cells):
        i = jnp.floor((cells + 0.5) * (1.0 / COLS))
        j = cells - i * COLS - 1.0
        return i, jnp.where(j < 0.0, COLS - 1.0, j)

    def fill_hot(hot_buf, j, lane_at):
        j16 = jnp.broadcast_to(j, (16, CN)).astype(bf16)
        for t in range(-(-COLS // 16)):
            hot_buf[16 * t : 16 * t + 16, lane_at : lane_at + CN] = jnp.where(
                row16 + jnp.full((16, CN), 16 * t, bf16) == j16, one, none
            )

    def build(g, left_buf, hot_buf):
        for n in range(GROUP):
            for slot in range(2):
                at = (2 * n + slot) * CN
                k = g * GROUP + n
                value = got_buf[k, 16 * slot : 16 * slot + 16, :]
                m = got_buf[k, 32 + slot : 33 + slot, :]
                i, j = place_of(got_buf[k, 34 + slot : 35 + slot, :])
                fill_hot(hot_buf, j, at)
                hi = value.astype(bf16)
                lo = (value - hi.astype(f32)).astype(bf16)
                i16 = jnp.broadcast_to(i, (16, CN)).astype(bf16)
                for r in range(ROWS):
                    mask = i16 == jnp.full((16, CN), r, bf16)
                    left_buf[16 * r : 16 * r + 16, at : at + CN] = jnp.where(mask, hi, none)
                    left_buf[160 + 16 * r : 176 + 16 * r, at : at + CN] = jnp.where(mask, lo, none)
                m16 = jnp.broadcast_to(m, (16, CN))
                mhi = m16.astype(bf16)
                mlo = (m16 - mhi.astype(f32)).astype(bf16)
                mask = i16 == row16
                left_buf[320:336, at : at + CN] = jnp.where(mask, mhi, none)
                left_buf[336:352, at : at + CN] = jnp.where(mask, mlo, none)

    def add_up(left_buf, hot_buf):
        acc_ref[...] += lax.dot_general(
            left_buf[...],
            hot_buf[...],
            (((1,), (1,)), ((), ())),
            preferred_element_type=f32,
        )

    def wait_for(g, skip=0):
        for n in range(skip, GROUP):
            p = g * GROUP + n
            pltpu.make_async_copy(out_buf.at[p], got_buf.at[p], recv_sem.at[p]).wait()

    even, odd = (left_bufs[0], hot_bufs[0]), (left_bufs[1], hot_bufs[1])
    groups = devices // GROUP

    def deposit_step(t, carry):
        wait_for(2 * t + 1)
        add_up(*even)
        build(2 * t + 1, *odd)
        wait_for(2 * t + 2)
        add_up(*odd)
        build(2 * t + 2, *even)
        return carry

    wait_for(0,1)
    wait_for(1)
    build(0,*even)
    build(1,*odd)
    add_up(*even)
    add_up(*odd)
    def ds(t,carry):
        wait_for(2 * t)
        wait_for(2 * t + 1)
        build(2*t,*even)
        build(2*t+1,*odd)
        add_up(*even)
        add_up(*odd)
        return carry
    lax.fori_loop(1, groups // 2, ds, 0)

    tile_ref[0:8, :] = acc_ref[320:328, :] + acc_ref[336:344, :]
    tile_ref[8:168, :] = acc_ref[0:160, :] + acc_ref[160:320, :]
    tile_ref[168:176, :] = acc_ref[328:336, :] + acc_ref[344:352, :]
    own, rest = tile_ref[:, 0:128], tile_ref[:, 128:256]
    at_lane = lax.broadcasted_iota(jnp.int32, (176, 128), 1)
    side_buf[0] = jnp.where(at_lane == 127, pltpu.roll(rest, 126, 1), own)
    side_buf[1] = jnp.where(at_lane == 0, rest, pltpu.roll(own, 2, 1))
    above, below = (wide + 15) % 16, (wide + 1) % 16
    before, after = (narrow + 7) % 8, (narrow + 1) % 8
    top, bottom = pl.ds(0, 40), pl.ds(136, 40)
    halo = [
        (tile_ref.at[top], up_buf.at[1], (above, narrow)),
        (tile_ref.at[bottom], up_buf.at[0], (below, narrow)),
        (side_buf.at[0], side_got.at[1], (wide, before)),
        (side_buf.at[1], side_got.at[0], (wide, after)),
        (side_buf.at[0, top], diag_got.at[3], (above, before)),
        (side_buf.at[0, bottom], diag_got.at[1], (below, before)),
        (side_buf.at[1, top], diag_got.at[2], (above, after)),
        (side_buf.at[1, bottom], diag_got.at[0], (below, after)),
    ]
    halo = [
        pltpu.make_async_remote_copy(
            src, dst, halo_send.at[n], halo_recv.at[n], device_id=to, device_id_type=MESH
        )
        for n, (src, dst, to) in enumerate(halo)
    ]
    for copy in halo:
        copy.start()
    for copy in halo:
        copy.wait()
    nothing = jnp.zeros((96, 128), f32)

    def with_corners(side, high, low):
        return side + jnp.concatenate(
            [high[32:40], high[0:32], nothing, low[8:40], low[0:8]], axis=0
        )

    from_left = with_corners(side_got[0], diag_got[0], diag_got[2])
    from_right = with_corners(side_got[1], diag_got[1], diag_got[3])
    high, low = up_buf[0], up_buf[1]
    nothing2 = jnp.zeros((96, 256), f32)
    vertical = jnp.concatenate(
        [high[32:40], high[0:32], nothing2, low[8:40], low[0:8]], axis=0
    )
    own = (
        own
        + vertical[:, 0:128]
        + jnp.where(at_lane == 0, from_left, 0.0)
        + jnp.where(at_lane == 127, from_right, 0.0)
    )
    rest = (
        rest
        + vertical[:, 128:256]
        + jnp.where(at_lane == 1, from_left, 0.0)
        + jnp.where(at_lane == 0, from_right, 0.0)
    )
    total = jnp.concatenate([own, rest], axis=1)
    for r in range(ROWS):
        at = r if r < 8 else 160 + r
        mean = total[8 + 16 * r : 24 + 16 * r, :] / (total[at : at + 1, :] + 1.0)
        if 1 <= r <= CW:
            mean_ref[:, r - 1, :] = mean[:, 0:CN]
        hi = mean.astype(bf16)
        mean_buf[16 * r : 16 * r + 16, :] = hi
        mean_buf[160 + 16 * r : 176 + 16 * r, :] = (mean - hi.astype(f32)).astype(bf16)

    def lookup(p, count, hot_buf):
        rows = []
        for n in range(count):
            for slot in range(2):
                i, j = place_of(got_buf[p + n, 34 + slot : 35 + slot, :])
                fill_hot(hot_buf, j, (2 * n + slot) * CN)
                rows.append(i)
        for n in range(count):
            found = jnp.dot(
                mean_buf[...],
                hot_buf[:, 256 * n : 256 * n + 256],
                preferred_element_type=f32,
            )
            for slot in range(2):
                i16 = jnp.broadcast_to(rows[2 * n + slot], (16, CN))
                near = jnp.zeros((16, CN), f32)
                cut = slice(CN * slot, CN * slot + CN)
                for r in range(ROWS):
                    near = near + jnp.where(
                        i16 == float(r),
                        found[16 * r : 16 * r + 16, cut] + found[160 + 16 * r : 176 + 16 * r, cut],
                        0.0,
                    )
                near_buf[2 * (p + n) + slot] = near

    def give_back(p, offset):
        pltpu.make_async_remote_copy(
            near_buf.at[pl.ds(2 * p, 2)],
            ret_buf.at[pl.ds(2 * me, 2)],
            back_send,
            back_recv.at[p],
            device_id=at_offset(offset, -1),
            device_id_type=MESH,
        ).start()

    def return_class(base, steps, offsets):
        def body(i, carry):
            listed = offsets(i)
            p = base + len(listed) * i
            for n in range(0, len(listed), 3):
                some = listed[n : n + 3]
                lookup(p + n, len(some), hot_bufs[(n // 3) % 2])
                for m, offset in enumerate(some):
                    give_back(p + n + m, offset)
            return carry

        lax.fori_loop(0, steps, body, 0)

    for arguments in reversed(classes):
        return_class(*arguments)
    for p in (8, 4, 0):
        lookup(p, min(4, 11 - p), hot_bufs[(p // 4) % 2])
        for n in range(p, min(p + 4, 11)):
            if n:
                give_back(n, near_by[n - 1])
    ret_buf[pl.ds(2 * me, 2)] = near_buf[0:2]

    def arrive(p, carry):
        pair = pl.ds(2 * p, 2)
        pltpu.make_async_copy(near_buf.at[pair], ret_buf.at[pair], back_recv.at[p]).wait()
        return carry

    lax.fori_loop(1, devices, arrive, 0)

    def read_rate(b, carry):
        p = idx_sm[4, b]
        row_buf[pl.ds(b, 1), :] = ret_buf[p, 0:1, :]
        return carry

    lax.fori_loop(0, lanes, read_rate, 0, unroll=4)
    row_buf[...] = jnp.exp(-freq_ref[...] * (1.5 + jnp.tanh(row_buf[...])))

    def mix(b, carry):
        p = idx_sm[4, b]
        near = ret_buf[p]
        mixed_ref[b] = near + (scal_ref[b] - near) * row_buf[pl.ds(b, 1), :]
        return carry

    lax.fori_loop(0, lanes, mix, 0, unroll=4)

    rest_of = pl.ds(1, devices - 1)
    pltpu.make_async_copy(out_buf.at[rest_of], got_buf.at[rest_of], send_sem).wait()
    rest_of = pl.ds(2, 2 * (devices - 1))
    pltpu.make_async_copy(near_buf.at[rest_of], ret_buf.at[rest_of], back_send).wait()


def per_device(scalars, mass, frequency, cell, owner):
    devices = lax.axis_size("wide") * lax.axis_size("narrow")
    blocks, count, per_block = scalars.shape
    f32, bf16 = jnp.float32, jnp.bfloat16
    vmem = pl.BlockSpec(memory_space=pltpu.VMEM)
    return pl.pallas_call(
        functools.partial(kernel, devices),
        out_shape=(
            jax.ShapeDtypeStruct((blocks, count, per_block), f32),
            jax.ShapeDtypeStruct((count, CW, CN), f32),
        ),
        in_specs=[pl.BlockSpec(memory_space=pltpu.HBM)] * 5,
        out_specs=(vmem, vmem),
        scratch_shapes=[
            pltpu.VMEM((devices, 36, per_block), f32),
            pltpu.VMEM((devices, 36, per_block), f32),
            pltpu.VMEM((2 * devices, 16, per_block), f32),
            pltpu.VMEM((2 * devices, 16, per_block), f32),
            pltpu.VMEM((blocks, count, per_block), f32),
            pltpu.VMEM((blocks, per_block), f32),
            pltpu.VMEM((blocks, per_block), jnp.int32),
            pltpu.VMEM((1, blocks), jnp.int32),
            pltpu.VMEM((352, GROUP * 256), bf16),
            pltpu.VMEM((352, GROUP * 256), bf16),
            pltpu.VMEM((256, GROUP * 256), bf16),
            pltpu.VMEM((256, GROUP * 256), bf16),
            pltpu.VMEM((352, 256), f32),
            pltpu.VMEM((176, 256), f32),
            pltpu.VMEM((2, 176, 128), f32),
            pltpu.VMEM((2, 40, 256), f32),
            pltpu.VMEM((2, 176, 128), f32),
            pltpu.VMEM((4, 40, 128), f32),
            pltpu.VMEM((320, 256), bf16),
            pltpu.VMEM((8, blocks), jnp.int32),
            pltpu.SMEM((8, blocks), jnp.int32),
            pltpu.VMEM((blocks, per_block), f32),
            pltpu.VMEM((blocks + 8, per_block), f32),
            pltpu.SemaphoreType.DMA((5,)),
            pltpu.SemaphoreType.REGULAR((3,)),
            pltpu.SemaphoreType.DMA,
            pltpu.SemaphoreType.DMA,
            pltpu.SemaphoreType.DMA((devices,)),
            pltpu.SemaphoreType.DMA,
            pltpu.SemaphoreType.DMA((devices,)),
            pltpu.SemaphoreType.DMA((8,)),
            pltpu.SemaphoreType.DMA((8,)),
        ],
        compiler_params=pltpu.CompilerParams(
            collective_id=0, has_side_effects=True, vmem_limit_bytes=64 << 20
        ),
        name="mixing",
    )(scalars, mass, frequency, cell, owner.reshape(1, blocks))


def solution(mesh):
    held = P(("wide", "narrow"), None)
    block = P(("wide", "narrow"), None, None)
    return jax.shard_map(
        per_device,
        mesh=mesh,
        in_specs=(block, held, held, held, held),
        out_specs=(block, P(None, "wide", "narrow")),
        check_vma=False,
    )
```

```python
import functools

import jax
import jax.numpy as jnp
from jax import lax
from jax.experimental import pallas as pl
from jax.experimental.pallas import tpu as pltpu
from jax.sharding import PartitionSpec as P

CW = 8
CN = 128
ROWS = CW + 2
COLS = CN + 2
MESH = pl.DeviceIdType.MESH
GROUP = 4
PAIR = 2 * GROUP
EARLY = 14


def kernel(
    devices,
    scal_hbm,
    mass_hbm,
    freq_hbm,
    cell_hbm,
    owner_hbm,
    mixed_ref,
    mean_ref,
    out_a,
    out_b,
    got_a,
    got_b,
    near_a,
    near_b,
    ret_a,
    ret_b,
    scal_ref,
    freq_ref,
    cell_ref,
    owner_ref,
    left_even,
    left_odd,
    hot_even,
    hot_odd,
    acc_a,
    acc_b,
    tile_a,
    tile_b,
    side_a,
    side_b,
    up_a,
    up_b,
    side_got_a,
    side_got_b,
    diag_a,
    diag_b,
    mean_a,
    mean_b,
    inverse_ref,
    idx_vm,
    idx_sm,
    row_buf,
    weight_ref,
    load_sem,
    hello_sem,
    idx_sem,
    send_sem,
    recv_sem,
    back_send,
    back_recv,
    halo_send,
    halo_recv,
):
    f32, bf16 = jnp.float32, jnp.bfloat16
    wide = lax.axis_index("wide")
    narrow = lax.axis_index("narrow")
    me = wide * 8 + narrow
    here = (lax.div(wide, 4), lax.rem(wide, 4), lax.div(narrow, 2), lax.rem(narrow, 2))

    def at_offset(offset, sign=1):
        z, x, y, c = (
            lax.rem(h + (d if sign > 0 else n - d), n) for h, d, n in zip(here, offset, (4, 4, 4, 2))
        )
        return z * 4 + x, y * 2 + c

    near_by = [(0, 0, 0, 1)]
    for d in (1, 3, 2):
        near_by += [(d, 0, 0, 0), (0, d, 0, 0), (0, 0, d, 0)]

    def two_axes(i):
        a, b = 1 + lax.div(i, 3), 1 + lax.rem(i, 3)
        on = [1 - lax.div(lax.rem(b - 1 + n, 3) + 1, 2) for n in (0, 2, 1)]
        return [(a, b, 0, 0), (b, 0, a, 0), (0, a, b, 0), (on[0] * a, on[1] * a, on[2] * a, 1)]

    def three_axes(i):
        a, b = 1 + lax.div(i, 3), 1 + lax.rem(i, 3)
        last = [(a, b, n, 0) for n in (1, 2, 3)]
        return [last[0], (a, b, 0, 1), last[1], (b, 0, a, 1), last[2], (0, a, b, 1)]

    def four_axes(i):
        a, b = 1 + lax.div(i, 3), 1 + lax.rem(i, 3)
        return [(a, b, n, 1) for n in (1, 2, 3)]

    classes = [(11, 9, two_axes), (47, 9, three_axes), (101, 9, four_axes)]

    def hello(sem):
        for offset in near_by:
            pl.semaphore_signal(sem, inc=1, device_id=at_offset(offset), device_id_type=MESH)

    barrier = pltpu.get_barrier_semaphore()
    hello(barrier)
    loads = [
        pltpu.make_async_copy(src, dst, load_sem.at[n])
        for n, (src, dst) in enumerate(
            (
                (owner_hbm, owner_ref),
                (scal_hbm, scal_ref),
                (mass_hbm, weight_ref.at[pl.ds(0, mass_hbm.shape[0])]),
                (cell_hbm, cell_ref),
                (freq_hbm, freq_ref),
            )
        )
    ]
    for copy in loads:
        copy.start()

    lanes = owner_ref.shape[1]
    weight_ref[lanes : lanes + 8, :] = jnp.zeros((8, CN), f32)
    acc_a[...] = jnp.zeros_like(acc_a)
    acc_b[...] = jnp.zeros_like(acc_b)
    for hot_buf in (hot_even, hot_odd):
        hot_buf[144:256, :] = jnp.zeros((112, hot_buf.shape[1]), bf16)
    loads[0].wait()
    along = jnp.broadcast_to(owner_ref[...], (lanes, lanes))
    down = along.T
    sub = lax.broadcasted_iota(jnp.int32, (lanes, lanes), 0)
    lane = lax.broadcasted_iota(jnp.int32, (lanes, lanes), 1)
    match = down == lane
    first = jnp.min(jnp.where(match, sub, lanes), axis=0, keepdims=True)
    second = jnp.max(jnp.where(match, sub, -1), axis=0, keepdims=True)
    earlier = jnp.where((down == along) & (sub < lane), 1, 0)
    place = 2 * owner_ref[...] + jnp.max(earlier, axis=0, keepdims=True)
    idx_vm[0:1, :] = jnp.minimum(first, lanes - 1)
    idx_vm[1:2, :] = jnp.maximum(second, 0)
    idx_vm[2:3, :] = first
    idx_vm[3:4, :] = jnp.where(second > first, second, lanes)
    idx_vm[4:5, :] = place
    idx_vm[5:8, :] = jnp.zeros((3, lanes), jnp.int32)
    to_scalar = pltpu.make_async_copy(idx_vm, idx_sm, idx_sem)
    to_scalar.start()
    to_scalar.wait()
    for copy in loads[1:]:
        copy.wait()

    outs, gots = (out_a, out_b), (got_a, got_b)
    nears, rets = (near_a, near_b), (ret_a, ret_b)
    accs, tiles, means = (acc_a, acc_b), (tile_a, tile_b), (mean_a, mean_b)

    def pack(half, dest, owner):
        for slot in range(2):
            b = idx_sm[slot, owner]
            m = weight_ref[pl.ds(idx_sm[2 + slot, owner], 1), :]
            dest[8 * slot : 8 * slot + 8, :] = scal_ref[b, 8 * half : 8 * half + 8, :] * m
            if half == 0:
                dest[16 + slot : 17 + slot, :] = m
                dest[18 + slot : 19 + slot, :] = cell_ref[pl.ds(b, 1), :].astype(f32)

    def send_to(half, p, offset):
        w, v = at_offset(offset)
        pack(half, outs[half].at[p], w * 8 + v)
        pltpu.make_async_remote_copy(
            outs[half].at[p],
            gots[half].at[p],
            send_sem.at[half],
            recv_sem.at[half, lax.div(p, PAIR)],
            device_id=(w, v),
            device_id_type=MESH,
        ).start()

    def send_class(half, base, steps, offsets):
        def body(i, carry):
            listed = offsets(i)
            for n, offset in enumerate(listed):
                send_to(half, base + len(listed) * i + n, offset)
            return carry

        lax.fori_loop(0, steps, body, 0)

    pl.semaphore_wait(barrier, len(near_by))
    hello(hello_sem.at[0])
    for n, offset in enumerate(near_by):
        send_to(0, 1 + n, offset)
    pl.semaphore_wait(hello_sem.at[0], len(near_by))
    hello(hello_sem.at[1])
    send_class(0, *classes[0])
    pl.semaphore_wait(hello_sem.at[1], len(near_by))
    hello(hello_sem.at[2])
    send_class(0, *classes[1])
    pl.semaphore_wait(hello_sem.at[2], len(near_by))
    send_class(0, *classes[2])
    pack(0, got_a.at[0], me)
    pack(1, got_b.at[0], me)
    for n, offset in enumerate(near_by):
        send_to(1, 1 + n, offset)
    for arguments in classes:
        send_class(1, *arguments)

    tile_row = lax.broadcasted_iota(jnp.int32, (16, CN), 0).astype(f32)
    row16 = tile_row.astype(bf16)
    none, one = jnp.zeros((16, CN), bf16), jnp.ones((16, CN), bf16)

    def place_of(cells):
        i = jnp.floor((cells + 0.5) * (1.0 / COLS))
        j = cells - i * COLS - 1.0
        return i, jnp.where(j < 0.0, COLS - 1.0, j)

    def fill_hot(hot_buf, j, lane_at):
        j16 = jnp.broadcast_to(j, (16, CN)).astype(bf16)
        for t in range(-(-COLS // 16)):
            hot_buf[16 * t : 16 * t + 16, lane_at : lane_at + CN] = jnp.where(
                row16 + jnp.full((16, CN), 16 * t, bf16) == j16, one, none
            )

    def two_terms(value):
        high = value.astype(bf16).astype(f32)
        return jnp.concatenate([high, value - high], axis=0).astype(bf16)

    def build(half, p0, left_buf, hot_buf):
        for n in range(GROUP):
            for slot in range(2):
                at = (2 * n + slot) * CN
                p = p0 + n
                i, j = place_of(got_a[p, 18 + slot : 19 + slot, :])
                fill_hot(hot_buf, j, at)
                terms = two_terms(gots[half][p, 8 * slot : 8 * slot + 8, :])
                i16 = jnp.broadcast_to(i, (16, CN)).astype(bf16)
                for r in range(ROWS):
                    left_buf[16 * r : 16 * r + 16, at : at + CN] = jnp.where(
                        i16 == jnp.full((16, CN), r, bf16), terms, none
                    )
                if half == 0:
                    m16 = jnp.broadcast_to(got_a[p, 16 + slot : 17 + slot, :], (16, CN))
                    mhi = m16.astype(bf16)
                    mlo = (m16 - mhi.astype(f32)).astype(bf16)
                    mask = i16 == row16
                    left_buf[160:176, at : at + CN] = jnp.where(mask, mhi, none)
                    left_buf[176:192, at : at + CN] = jnp.where(mask, mlo, none)

    def add_up(half, left_buf, hot_buf):
        rows = accs[half].shape[0]
        accs[half][...] += lax.dot_general(
            left_buf[0:rows, :],
            hot_buf[...],
            (((1,), (1,)), ((), ())),
            preferred_element_type=f32,
        )

    def deposit(half, t, first=0):
        p = t * PAIR
        span = pl.ds(p + first, PAIR - first)
        pltpu.make_async_copy(
            outs[half].at[span], gots[half].at[span], recv_sem.at[half, t]
        ).wait()
        build(half, p, left_even, hot_even)
        build(half, p + GROUP, left_odd, hot_odd)
        add_up(half, left_even, hot_even)
        add_up(half, left_odd, hot_odd)

    def deposit_range(half, low, high):
        def body(t, carry):
            deposit(half, t)
            return carry

        lax.fori_loop(low, high, body, 0)

    above, below = (wide + 15) % 16, (wide + 1) % 16
    before, after = (narrow + 7) % 8, (narrow + 1) % 8
    at_lanes = [
        lax.broadcasted_iota(jnp.int32, (tile.shape[0], 128), 1) for tile in tiles
    ]

    def halo_copies(half):
        tile_ref, side_buf = tiles[half], (side_a, side_b)[half]
        up, side_got, diag = ((up_a, side_got_a, diag_a), (up_b, side_got_b, diag_b))[half]
        rows, edge = tile_ref.shape[0], up.shape[1]
        top, bottom = pl.ds(0, edge), pl.ds(rows - edge, edge)
        listed = [
            (tile_ref.at[top], up.at[1], (above, narrow)),
            (tile_ref.at[bottom], up.at[0], (below, narrow)),
            (side_buf.at[0], side_got.at[1], (wide, before)),
            (side_buf.at[1], side_got.at[0], (wide, after)),
            (side_buf.at[0, top], diag.at[3], (above, before)),
            (side_buf.at[0, bottom], diag.at[1], (below, before)),
            (side_buf.at[1, top], diag.at[2], (above, after)),
            (side_buf.at[1, bottom], diag.at[0], (below, after)),
        ]
        return [
            pltpu.make_async_remote_copy(
                src,
                dst,
                halo_send.at[half, n],
                halo_recv.at[half, n],
                device_id=to,
                device_id_type=MESH,
            )
            for n, (src, dst, to) in enumerate(listed)
        ]

    def halo_start(half):
        acc, tile_ref, side_buf = accs[half], tiles[half], (side_a, side_b)[half]
        start = 8 if half == 0 else 0
        for r in range(ROWS):
            tile_ref[start + 8 * r : start + 8 * r + 8, :] = (
                acc[16 * r : 16 * r + 8, :] + acc[16 * r + 8 : 16 * r + 16, :]
            )
        if half == 0:
            tile_ref[0:8, :] = acc[160:168, :] + acc[176:184, :]
            tile_ref[88:96, :] = acc[168:176, :] + acc[184:192, :]
        own, rest = tile_ref[:, 0:128], tile_ref[:, 128:256]
        at_lane = at_lanes[half]
        side_buf[0] = jnp.where(at_lane == 127, pltpu.roll(rest, 126, 1), own)
        side_buf[1] = jnp.where(at_lane == 0, rest, pltpu.roll(own, 2, 1))
        for copy in halo_copies(half):
            copy.start()

    def halo_finish(half):
        for copy in halo_copies(half):
            copy.wait()
        tile_ref, at_lane = tiles[half], at_lanes[half]
        up, side_got, diag = ((up_a, side_got_a, diag_a), (up_b, side_got_b, diag_b))[half]

        def unfold(high, low):
            middle = jnp.zeros((48, high.shape[1]), f32)
            if half == 0:
                parts = [high[16:24], high[0:16], middle, low[8:24], low[0:8]]
            else:
                parts = [high, middle, low]
            return jnp.concatenate(parts, axis=0)

        from_left = side_got[0] + unfold(diag[0], diag[2])
        from_right = side_got[1] + unfold(diag[1], diag[3])
        vertical = unfold(up[0], up[1])
        own = (
            tile_ref[:, 0:128]
            + vertical[:, 0:128]
            + jnp.where(at_lane == 0, from_left, 0.0)
            + jnp.where(at_lane == 127, from_right, 0.0)
        )
        rest = (
            tile_ref[:, 128:256]
            + vertical[:, 128:256]
            + jnp.where(at_lane == 1, from_left, 0.0)
            + jnp.where(at_lane == 0, from_right, 0.0)
        )
        total = jnp.concatenate([own, rest], axis=1)
        if half == 0:
            inverse_ref[0:8, :] = 1.0 / (total[0:8, :] + 1.0)
            inverse_ref[8:16, :] = 1.0 / (total[88:96, :] + 1.0)
        start = 8 if half == 0 else 0
        for r in range(ROWS):
            mean = total[start + 8 * r : start + 8 * r + 8, :] * inverse_ref[r : r + 1, :]
            if 1 <= r <= CW:
                mean_ref[8 * half : 8 * half + 8, r - 1, :] = mean[:, 0:CN]
            means[half][16 * r : 16 * r + 16, :] = two_terms(mean)

    def lookup(half, p, count, hot_buf):
        rows = []
        for n in range(count):
            for slot in range(2):
                i, j = place_of(got_a[p + n, 18 + slot : 19 + slot, :])
                fill_hot(hot_buf, j, (2 * n + slot) * CN)
                rows.append(i)
        for n in range(count):
            found = jnp.dot(
                means[half][...],
                hot_buf[:, 256 * n : 256 * n + 256],
                preferred_element_type=f32,
            )
            for slot in range(2):
                i8 = jnp.broadcast_to(rows[2 * n + slot], (8, CN))
                near = jnp.zeros((8, CN), f32)
                cut = slice(CN * slot, CN * slot + CN)
                for r in range(ROWS):
                    near = near + jnp.where(
                        i8 == float(r),
                        found[16 * r : 16 * r + 8, cut] + found[16 * r + 8 : 16 * r + 16, cut],
                        0.0,
                    )
                nears[half][2 * (p + n) + slot] = near

    def give_back(half, p, offset):
        pltpu.make_async_remote_copy(
            nears[half].at[pl.ds(2 * p, 2)],
            rets[half].at[pl.ds(2 * me, 2)],
            back_send.at[half],
            back_recv.at[half],
            device_id=at_offset(offset, -1),
            device_id_type=MESH,
        ).start()

    hot_bufs = (hot_even, hot_odd)

    def return_class(half, base, steps, offsets):
        def body(i, carry):
            listed = offsets(i)
            p = base + len(listed) * i
            for n in range(0, len(listed), 3):
                some = listed[n : n + 3]
                lookup(half, p + n, len(some), hot_bufs[(n // 3) % 2])
                for m, offset in enumerate(some):
                    give_back(half, p + n + m, offset)
            return carry

        lax.fori_loop(0, steps, body, 0)

    def return_near(half):
        for p in (8, 4, 0):
            lookup(half, p, min(4, 11 - p), hot_bufs[(p // 4) % 2])
            for n in range(p, min(p + 4, 11)):
                if n:
                    give_back(half, n, near_by[n - 1])
        rets[half][pl.ds(2 * me, 2)] = nears[half][0:2]

    pairs = devices // PAIR
    deposit(0, 0, 1)
    deposit_range(0, 1, pairs)
    halo_start(0)
    deposit(1, 0, 1)
    deposit_range(1, 1, EARLY)
    halo_finish(0)
    return_class(0, *classes[2])
    return_class(0, *classes[1])
    deposit_range(1, EARLY, pairs)
    halo_start(1)
    return_class(0, *classes[0])
    return_near(0)
    halo_finish(1)
    for arguments in reversed(classes):
        return_class(1, *arguments)
    return_near(1)

    others = pl.ds(2, 2 * (devices - 1))

    def returned(half):
        pltpu.make_async_copy(
            nears[half].at[others], rets[half].at[others], back_recv.at[half]
        ).wait()

    returned(0)

    def read_rate(b, carry):
        row_buf[pl.ds(b, 1), :] = ret_a[idx_sm[4, b], 0:1, :]
        return carry

    lax.fori_loop(0, lanes, read_rate, 0, unroll=8)
    row_buf[...] = jnp.exp(-freq_ref[...] * (1.5 + jnp.tanh(row_buf[...])))

    def mix(half):
        def body(b, carry):
            near = rets[half][idx_sm[4, b]]
            own = scal_ref[b, 8 * half : 8 * half + 8, :]
            mixed_ref[b, 8 * half : 8 * half + 8, :] = near + (own - near) * row_buf[pl.ds(b, 1), :]
            return carry

        lax.fori_loop(0, lanes, body, 0, unroll=8)

    mix(0)
    returned(1)
    mix(1)

    for half in range(2):
        rest_of = pl.ds(1, devices - 1)
        pltpu.make_async_copy(
            outs[half].at[rest_of], gots[half].at[rest_of], send_sem.at[half]
        ).wait()
        pltpu.make_async_copy(
            nears[half].at[others], rets[half].at[others], back_send.at[half]
        ).wait()


def per_device(scalars, mass, frequency, cell, owner):
    devices = lax.axis_size("wide") * lax.axis_size("narrow")
    blocks, count, per_block = scalars.shape
    f32, bf16 = jnp.float32, jnp.bfloat16
    vmem = pl.BlockSpec(memory_space=pltpu.VMEM)
    return pl.pallas_call(
        functools.partial(kernel, devices),
        out_shape=(
            jax.ShapeDtypeStruct((blocks, count, per_block), f32),
            jax.ShapeDtypeStruct((count, CW, CN), f32),
        ),
        in_specs=[pl.BlockSpec(memory_space=pltpu.HBM)] * 5,
        out_specs=(vmem, vmem),
        scratch_shapes=[
            pltpu.VMEM((devices, 20, per_block), f32),
            pltpu.VMEM((devices, 16, per_block), f32),
            pltpu.VMEM((devices, 20, per_block), f32),
            pltpu.VMEM((devices, 16, per_block), f32),
            *[pltpu.VMEM((2 * devices, 8, per_block), f32)] * 4,
            pltpu.VMEM((blocks, count, per_block), f32),
            pltpu.VMEM((blocks, per_block), f32),
            pltpu.VMEM((blocks, per_block), jnp.int32),
            pltpu.VMEM((1, blocks), jnp.int32),
            pltpu.VMEM((192, GROUP * 256), bf16),
            pltpu.VMEM((192, GROUP * 256), bf16),
            pltpu.VMEM((256, GROUP * 256), bf16),
            pltpu.VMEM((256, GROUP * 256), bf16),
            pltpu.VMEM((192, 256), f32),
            pltpu.VMEM((160, 256), f32),
            pltpu.VMEM((96, 256), f32),
            pltpu.VMEM((80, 256), f32),
            pltpu.VMEM((2, 96, 128), f32),
            pltpu.VMEM((2, 80, 128), f32),
            pltpu.VMEM((2, 24, 256), f32),
            pltpu.VMEM((2, 16, 256), f32),
            pltpu.VMEM((2, 96, 128), f32),
            pltpu.VMEM((2, 80, 128), f32),
            pltpu.VMEM((4, 24, 128), f32),
            pltpu.VMEM((4, 16, 128), f32),
            pltpu.VMEM((160, 256), bf16),
            pltpu.VMEM((160, 256), bf16),
            pltpu.VMEM((16, 256), f32),
            pltpu.VMEM((8, blocks), jnp.int32),
            pltpu.SMEM((8, blocks), jnp.int32),
            pltpu.VMEM((blocks, per_block), f32),
            pltpu.VMEM((blocks + 8, per_block), f32),
            pltpu.SemaphoreType.DMA((5,)),
            pltpu.SemaphoreType.REGULAR((3,)),
            pltpu.SemaphoreType.DMA,
            pltpu.SemaphoreType.DMA((2,)),
            pltpu.SemaphoreType.DMA((2, devices // PAIR)),
            pltpu.SemaphoreType.DMA((2,)),
            pltpu.SemaphoreType.DMA((2,)),
            pltpu.SemaphoreType.DMA((2, 8)),
            pltpu.SemaphoreType.DMA((2, 8)),
        ],
        compiler_params=pltpu.CompilerParams(
            collective_id=0, has_side_effects=True, vmem_limit_bytes=64 << 20
        ),
        name="mixing",
    )(scalars, mass, frequency, cell, owner.reshape(1, blocks))


def solution(mesh):
    held = P(("wide", "narrow"), None)
    block = P(("wide", "narrow"), None, None)
    return jax.shard_map(
        per_device,
        mesh=mesh,
        in_specs=(block, held, held, held, held),
        out_specs=(block, P(None, "wide", "narrow")),
        check_vma=False,
    )
```

```python
import functools

import jax
import jax.numpy as jnp
from jax import lax
from jax.experimental import pallas as pl
from jax.experimental.pallas import tpu as pltpu
from jax.sharding import PartitionSpec as P

CW = 8
CN = 128
ROWS = CW + 2
COLS = CN + 2
MESH = pl.DeviceIdType.MESH
GROUP = 4
PAIR = 2 * GROUP
EARLY = 11


def kernel(
    devices,
    scal_hbm,
    mass_hbm,
    freq_hbm,
    cell_hbm,
    owner_hbm,
    mixed_ref,
    mean_ref,
    out_a,
    out_b,
    got_a,
    got_b,
    near_a,
    near_b,
    ret_a,
    ret_b,
    scal_ref,
    freq_ref,
    cell_ref,
    owner_ref,
    left_even,
    left_odd,
    hot_ref,
    acc_a,
    acc_b,
    tile_a,
    tile_b,
    side_a,
    side_b,
    up_a,
    up_b,
    side_got_a,
    side_got_b,
    diag_a,
    diag_b,
    mean_a,
    mean_b,
    inverse_ref,
    idx_vm,
    idx_sm,
    row_buf,
    weight_ref,
    load_sem,
    hello_sem,
    idx_sem,
    send_sem,
    recv_sem,
    back_send,
    back_recv,
    halo_send,
    halo_recv,
):
    f32, bf16 = jnp.float32, jnp.bfloat16
    wide = lax.axis_index("wide")
    narrow = lax.axis_index("narrow")
    me = wide * 8 + narrow
    here = (lax.div(wide, 4), lax.rem(wide, 4), lax.div(narrow, 2), lax.rem(narrow, 2))

    def at_offset(offset, sign=1):
        z, x, y, c = (
            lax.rem(h + (d if sign > 0 else n - d), n) for h, d, n in zip(here, offset, (4, 4, 4, 2))
        )
        return z * 4 + x, y * 2 + c

    near_by = [(0, 0, 0, 1)]
    for d in (1, 3, 2):
        near_by += [(d, 0, 0, 0), (0, d, 0, 0), (0, 0, d, 0)]

    def two_axes(i):
        a, b = 1 + lax.div(i, 3), 1 + lax.rem(i, 3)
        on = [1 - lax.div(lax.rem(b - 1 + n, 3) + 1, 2) for n in (0, 2, 1)]
        return [(a, b, 0, 0), (b, 0, a, 0), (0, a, b, 0), (on[0] * a, on[1] * a, on[2] * a, 1)]

    def three_axes(i):
        a, b = 1 + lax.div(i, 3), 1 + lax.rem(i, 3)
        last = [(a, b, n, 0) for n in (1, 2, 3)]
        return [last[0], (a, b, 0, 1), last[1], (b, 0, a, 1), last[2], (0, a, b, 1)]

    def four_axes(i):
        a = 1 + i
        return [(a, b, 1 + (b + n) % 3, 1) for n in range(3) for b in (1, 2, 3)]

    classes = [(11, 9, two_axes), (47, 9, three_axes), (101, 3, four_axes)]

    def hello(sem):
        for offset in near_by:
            pl.semaphore_signal(sem, inc=1, device_id=at_offset(offset), device_id_type=MESH)

    barrier = pltpu.get_barrier_semaphore()
    hello(barrier)
    loads = [
        pltpu.make_async_copy(src, dst, load_sem.at[n])
        for n, (src, dst) in enumerate(
            (
                (owner_hbm, owner_ref),
                (scal_hbm, scal_ref),
                (mass_hbm, weight_ref.at[pl.ds(0, mass_hbm.shape[0])]),
                (cell_hbm, cell_ref),
                (freq_hbm, freq_ref),
            )
        )
    ]
    for copy in loads:
        copy.start()

    lanes = owner_ref.shape[1]
    weight_ref[lanes : lanes + 8, :] = jnp.zeros((8, CN), f32)
    acc_a[...] = jnp.zeros_like(acc_a)
    acc_b[...] = jnp.zeros_like(acc_b)
    loads[0].wait()
    along = jnp.broadcast_to(owner_ref[...], (lanes, lanes))
    down = along.T
    sub = lax.broadcasted_iota(jnp.int32, (lanes, lanes), 0)
    lane = lax.broadcasted_iota(jnp.int32, (lanes, lanes), 1)
    match = down == lane
    first = jnp.min(jnp.where(match, sub, lanes), axis=0, keepdims=True)
    second = jnp.max(jnp.where(match, sub, -1), axis=0, keepdims=True)
    earlier = jnp.where((down == along) & (sub < lane), 1, 0)
    place = 2 * owner_ref[...] + jnp.max(earlier, axis=0, keepdims=True)
    idx_vm[0:1, :] = jnp.minimum(first, lanes - 1)
    idx_vm[1:2, :] = jnp.maximum(second, 0)
    idx_vm[2:3, :] = first
    idx_vm[3:4, :] = jnp.where(second > first, second, lanes)
    idx_vm[4:5, :] = place
    idx_vm[5:8, :] = jnp.zeros((3, lanes), jnp.int32)
    to_scalar = pltpu.make_async_copy(idx_vm, idx_sm, idx_sem)
    to_scalar.start()
    to_scalar.wait()
    for copy in loads[1:]:
        copy.wait()

    outs, gots = (out_a, out_b), (got_a, got_b)
    nears, rets = (near_a, near_b), (ret_a, ret_b)
    accs, tiles, means = (acc_a, acc_b), (tile_a, tile_b), (mean_a, mean_b)

    def pack(half, dest, owner):
        for slot in range(2):
            b = idx_sm[slot, owner]
            m = weight_ref[pl.ds(idx_sm[2 + slot, owner], 1), :]
            dest[8 * slot : 8 * slot + 8, :] = scal_ref[b, 8 * half : 8 * half + 8, :] * m
            if half == 0:
                dest[16 + slot : 17 + slot, :] = m
                dest[18 + slot : 19 + slot, :] = cell_ref[pl.ds(b, 1), :].astype(f32)

    def send_to(half, p, offset):
        w, v = at_offset(offset)
        pack(half, outs[half].at[p], w * 8 + v)
        pltpu.make_async_remote_copy(
            outs[half].at[p],
            gots[half].at[p],
            send_sem.at[half],
            recv_sem.at[half, lax.div(p, PAIR)],
            device_id=(w, v),
            device_id_type=MESH,
        ).start()

    def send_class(half, base, steps, offsets):
        def body(i, carry):
            listed = offsets(i)
            for n, offset in enumerate(listed):
                send_to(half, base + len(listed) * i + n, offset)
            return carry

        lax.fori_loop(0, steps, body, 0)

    pl.semaphore_wait(barrier, len(near_by))
    hello(hello_sem.at[0])
    for n, offset in enumerate(near_by):
        send_to(0, 1 + n, offset)
    pl.semaphore_wait(hello_sem.at[0], len(near_by))
    hello(hello_sem.at[1])
    send_class(0, *classes[0])
    pl.semaphore_wait(hello_sem.at[1], len(near_by))
    hello(hello_sem.at[2])
    send_class(0, *classes[1])
    pl.semaphore_wait(hello_sem.at[2], len(near_by))
    send_class(0, *classes[2])
    pack(0, got_a.at[0], me)
    pack(1, got_b.at[0], me)
    for n, offset in enumerate(near_by):
        send_to(1, 1 + n, offset)
    for arguments in classes:
        send_class(1, *arguments)

    tile_row = lax.broadcasted_iota(jnp.int32, (16, CN), 0).astype(f32)
    row16 = tile_row.astype(bf16)
    none, one = jnp.zeros((16, CN), bf16), jnp.ones((16, CN), bf16)

    def place_of(cells):
        i = jnp.floor((cells + 0.5) * (1.0 / COLS))
        j = cells - i * COLS - 1.0
        return i, jnp.where(j < 0.0, COLS - 1.0, j)

    def fill_hot(p, slot, j):
        j16 = jnp.broadcast_to(j, (16, CN)).astype(bf16)
        for t in range(-(-COLS // 16)):
            hot_ref[p, 16 * t : 16 * t + 16, CN * slot : CN * slot + CN] = jnp.where(
                row16 + jnp.full((16, CN), 16 * t, bf16) == j16, one, none
            )

    def two_terms(value):
        high = value.astype(bf16).astype(f32)
        return jnp.concatenate([high, value - high], axis=0).astype(bf16)

    def build(half, p0, left_buf):
        for n in range(GROUP):
            for slot in range(2):
                at = (2 * n + slot) * CN
                p = p0 + n
                i, j = place_of(got_a[p, 18 + slot : 19 + slot, :])
                if half == 0:
                    fill_hot(p, slot, j)
                terms = two_terms(gots[half][p, 8 * slot : 8 * slot + 8, :])
                i16 = jnp.broadcast_to(i, (16, CN)).astype(bf16)
                for r in range(ROWS):
                    left_buf[16 * r : 16 * r + 16, at : at + CN] = jnp.where(
                        i16 == jnp.full((16, CN), r, bf16), terms, none
                    )
                if half == 0:
                    m16 = jnp.broadcast_to(got_a[p, 16 + slot : 17 + slot, :], (16, CN))
                    mhi = m16.astype(bf16)
                    mlo = (m16 - mhi.astype(f32)).astype(bf16)
                    mask = i16 == row16
                    left_buf[160:176, at : at + CN] = jnp.where(mask, mhi, none)
                    left_buf[176:192, at : at + CN] = jnp.where(mask, mlo, none)

    def add_up(half, p0, left_buf):
        rows = accs[half].shape[0]
        for n in range(GROUP):
            accs[half][:, 0:144] += lax.dot_general(
                left_buf[0:rows, 256 * n : 256 * n + 256],
                hot_ref[p0 + n],
                (((1,), (1,)), ((), ())),
                preferred_element_type=f32,
            )

    def deposit(half, t, first=0):
        p = t * PAIR
        span = pl.ds(p + first, PAIR - first)
        pltpu.make_async_copy(
            outs[half].at[span], gots[half].at[span], recv_sem.at[half, t]
        ).wait()
        build(half, p, left_even)
        build(half, p + GROUP, left_odd)
        add_up(half, p, left_even)
        add_up(half, p + GROUP, left_odd)

    def deposit_range(half, low, high):
        def body(t, carry):
            deposit(half, t)
            return carry

        lax.fori_loop(low, high, body, 0)

    above, below = (wide + 15) % 16, (wide + 1) % 16
    before, after = (narrow + 7) % 8, (narrow + 1) % 8
    at_lanes = [
        lax.broadcasted_iota(jnp.int32, (tile.shape[0], 128), 1) for tile in tiles
    ]

    def halo_copies(half):
        tile_ref, side_buf = tiles[half], (side_a, side_b)[half]
        up, side_got, diag = ((up_a, side_got_a, diag_a), (up_b, side_got_b, diag_b))[half]
        rows, edge = tile_ref.shape[0], up.shape[1]
        top, bottom = pl.ds(0, edge), pl.ds(rows - edge, edge)
        listed = [
            (tile_ref.at[top], up.at[1], (above, narrow)),
            (tile_ref.at[bottom], up.at[0], (below, narrow)),
            (side_buf.at[0], side_got.at[1], (wide, before)),
            (side_buf.at[1], side_got.at[0], (wide, after)),
            (side_buf.at[0, top], diag.at[3], (above, before)),
            (side_buf.at[0, bottom], diag.at[1], (below, before)),
            (side_buf.at[1, top], diag.at[2], (above, after)),
            (side_buf.at[1, bottom], diag.at[0], (below, after)),
        ]
        return [
            pltpu.make_async_remote_copy(
                src,
                dst,
                halo_send.at[half, n],
                halo_recv.at[half, n],
                device_id=to,
                device_id_type=MESH,
            )
            for n, (src, dst, to) in enumerate(listed)
        ]

    def halo_start(half):
        acc, tile_ref, side_buf = accs[half], tiles[half], (side_a, side_b)[half]
        start = 8 if half == 0 else 0
        for r in range(ROWS):
            tile_ref[start + 8 * r : start + 8 * r + 8, :] = (
                acc[16 * r : 16 * r + 8, :] + acc[16 * r + 8 : 16 * r + 16, :]
            )
        if half == 0:
            tile_ref[0:8, :] = acc[160:168, :] + acc[176:184, :]
            tile_ref[88:96, :] = acc[168:176, :] + acc[184:192, :]
        own, rest = tile_ref[:, 0:128], tile_ref[:, 128:256]
        at_lane = at_lanes[half]
        side_buf[0] = jnp.where(at_lane == 127, pltpu.roll(rest, 126, 1), own)
        side_buf[1] = jnp.where(at_lane == 0, rest, pltpu.roll(own, 2, 1))
        for copy in halo_copies(half):
            copy.start()

    def halo_finish(half):
        for copy in halo_copies(half):
            copy.wait()
        tile_ref, at_lane = tiles[half], at_lanes[half]
        up, side_got, diag = ((up_a, side_got_a, diag_a), (up_b, side_got_b, diag_b))[half]

        def unfold(high, low):
            middle = jnp.zeros((48, high.shape[1]), f32)
            if half == 0:
                parts = [high[16:24], high[0:16], middle, low[8:24], low[0:8]]
            else:
                parts = [high, middle, low]
            return jnp.concatenate(parts, axis=0)

        from_left = side_got[0] + unfold(diag[0], diag[2])
        from_right = side_got[1] + unfold(diag[1], diag[3])
        vertical = unfold(up[0], up[1])
        own = (
            tile_ref[:, 0:128]
            + vertical[:, 0:128]
            + jnp.where(at_lane == 0, from_left, 0.0)
            + jnp.where(at_lane == 127, from_right, 0.0)
        )
        rest = (
            tile_ref[:, 128:256]
            + vertical[:, 128:256]
            + jnp.where(at_lane == 1, from_left, 0.0)
            + jnp.where(at_lane == 0, from_right, 0.0)
        )
        total = jnp.concatenate([own, rest], axis=1)
        if half == 0:
            inverse_ref[0:8, :] = 1.0 / (total[0:8, :] + 1.0)
            inverse_ref[8:16, :] = 1.0 / (total[88:96, :] + 1.0)
        start = 8 if half == 0 else 0
        for r in range(ROWS):
            mean = total[start + 8 * r : start + 8 * r + 8, :] * inverse_ref[r : r + 1, :]
            if 1 <= r <= CW:
                mean_ref[8 * half : 8 * half + 8, r - 1, :] = mean[:, 0:CN]
            means[half][16 * r : 16 * r + 16, :] = two_terms(mean)

    def lookup(half, p, count):
        for n in range(count):
            found = jnp.dot(
                means[half][:, 0:144], hot_ref[p + n], preferred_element_type=f32
            )
            for slot in range(2):
                i, _ = place_of(got_a[p + n, 18 + slot : 19 + slot, :])
                i16 = jnp.broadcast_to(i, (16, CN))
                cut = slice(CN * slot, CN * slot + CN)
                near = found[0:16, cut]
                for r in range(1, ROWS):
                    near = jnp.where(i16 == float(r), found[16 * r : 16 * r + 16, cut], near)
                nears[half][2 * (p + n) + slot] = near[0:8] + near[8:16]

    def give_back(half, p, offset):
        pltpu.make_async_remote_copy(
            nears[half].at[pl.ds(2 * p, 2)],
            rets[half].at[pl.ds(2 * me, 2)],
            back_send.at[half],
            back_recv.at[half],
            device_id=at_offset(offset, -1),
            device_id_type=MESH,
        ).start()

    def return_class(half, base, steps, offsets):
        def body(i, carry):
            listed = offsets(i)
            p = base + len(listed) * i
            lookup(half, p, len(listed))
            for n, offset in enumerate(listed):
                give_back(half, p + n, offset)
            return carry

        lax.fori_loop(0, steps, body, 0)

    def return_near(half):
        for p in (8, 4, 0):
            lookup(half, p, min(4, 11 - p))
            for n in range(p, min(p + 4, 11)):
                if n:
                    give_back(half, n, near_by[n - 1])
        rets[half][pl.ds(2 * me, 2)] = nears[half][0:2]

    pairs = devices // PAIR
    deposit(0, 0, 1)
    deposit_range(0, 1, pairs)
    halo_start(0)
    deposit(1, 0, 1)
    deposit_range(1, 1, EARLY)
    halo_finish(0)
    return_class(0, *classes[2])
    return_class(0, *classes[1])
    deposit_range(1, EARLY, pairs)
    halo_start(1)
    return_class(0, *classes[0])
    return_near(0)
    halo_finish(1)
    for arguments in reversed(classes):
        return_class(1, *arguments)
    return_near(1)

    others = pl.ds(2, 2 * (devices - 1))

    def returned(half):
        pltpu.make_async_copy(
            nears[half].at[others], rets[half].at[others], back_recv.at[half]
        ).wait()

    returned(0)

    def read_rate(b, carry):
        row_buf[pl.ds(b, 1), :] = ret_a[idx_sm[4, b], 0:1, :]
        return carry

    lax.fori_loop(0, lanes, read_rate, 0, unroll=8)
    row_buf[...] = jnp.exp(-freq_ref[...] * (1.5 + jnp.tanh(row_buf[...])))

    def mix(half):
        def body(b, carry):
            near = rets[half][idx_sm[4, b]]
            own = scal_ref[b, 8 * half : 8 * half + 8, :]
            mixed_ref[b, 8 * half : 8 * half + 8, :] = near + (own - near) * row_buf[pl.ds(b, 1), :]
            return carry

        lax.fori_loop(0, lanes, body, 0, unroll=8)

    mix(0)
    returned(1)
    mix(1)

    for half in range(2):
        rest_of = pl.ds(1, devices - 1)
        pltpu.make_async_copy(
            outs[half].at[rest_of], gots[half].at[rest_of], send_sem.at[half]
        ).wait()
        pltpu.make_async_copy(
            nears[half].at[others], rets[half].at[others], back_send.at[half]
        ).wait()


def per_device(scalars, mass, frequency, cell, owner):
    devices = lax.axis_size("wide") * lax.axis_size("narrow")
    blocks, count, per_block = scalars.shape
    f32, bf16 = jnp.float32, jnp.bfloat16
    vmem = pl.BlockSpec(memory_space=pltpu.VMEM)
    return pl.pallas_call(
        functools.partial(kernel, devices),
        out_shape=(
            jax.ShapeDtypeStruct((blocks, count, per_block), f32),
            jax.ShapeDtypeStruct((count, CW, CN), f32),
        ),
        in_specs=[pl.BlockSpec(memory_space=pltpu.HBM)] * 5,
        out_specs=(vmem, vmem),
        scratch_shapes=[
            pltpu.VMEM((devices, 20, per_block), f32),
            pltpu.VMEM((devices, 16, per_block), f32),
            pltpu.VMEM((devices, 20, per_block), f32),
            pltpu.VMEM((devices, 16, per_block), f32),
            *[pltpu.VMEM((2 * devices, 8, per_block), f32)] * 4,
            pltpu.VMEM((blocks, count, per_block), f32),
            pltpu.VMEM((blocks, per_block), f32),
            pltpu.VMEM((blocks, per_block), jnp.int32),
            pltpu.VMEM((1, blocks), jnp.int32),
            pltpu.VMEM((192, GROUP * 256), bf16),
            pltpu.VMEM((192, GROUP * 256), bf16),
            pltpu.VMEM((devices, 144, 256), bf16),
            pltpu.VMEM((192, 256), f32),
            pltpu.VMEM((160, 256), f32),
            pltpu.VMEM((96, 256), f32),
            pltpu.VMEM((80, 256), f32),
            pltpu.VMEM((2, 96, 128), f32),
            pltpu.VMEM((2, 80, 128), f32),
            pltpu.VMEM((2, 24, 256), f32),
            pltpu.VMEM((2, 16, 256), f32),
            pltpu.VMEM((2, 96, 128), f32),
            pltpu.VMEM((2, 80, 128), f32),
            pltpu.VMEM((4, 24, 128), f32),
            pltpu.VMEM((4, 16, 128), f32),
            pltpu.VMEM((160, 256), bf16),
            pltpu.VMEM((160, 256), bf16),
            pltpu.VMEM((16, 256), f32),
            pltpu.VMEM((8, blocks), jnp.int32),
            pltpu.SMEM((8, blocks), jnp.int32),
            pltpu.VMEM((blocks, per_block), f32),
            pltpu.VMEM((blocks + 8, per_block), f32),
            pltpu.SemaphoreType.DMA((5,)),
            pltpu.SemaphoreType.REGULAR((3,)),
            pltpu.SemaphoreType.DMA,
            pltpu.SemaphoreType.DMA((2,)),
            pltpu.SemaphoreType.DMA((2, devices // PAIR)),
            pltpu.SemaphoreType.DMA((2,)),
            pltpu.SemaphoreType.DMA((2,)),
            pltpu.SemaphoreType.DMA((2, 8)),
            pltpu.SemaphoreType.DMA((2, 8)),
        ],
        compiler_params=pltpu.CompilerParams(
            collective_id=0, has_side_effects=True, vmem_limit_bytes=64 << 20
        ),
        name="mixing",
    )(scalars, mass, frequency, cell, owner.reshape(1, blocks))


def solution(mesh):
    held = P(("wide", "narrow"), None)
    block = P(("wide", "narrow"), None, None)
    return jax.shard_map(
        per_device,
        mesh=mesh,
        in_specs=(block, held, held, held, held),
        out_specs=(block, P(None, "wide", "narrow")),
        check_vma=False,
    )
```

```python
import functools

import jax
import jax.numpy as jnp
from jax import lax
from jax.experimental import pallas as pl
from jax.experimental.pallas import tpu as pltpu
from jax.sharding import PartitionSpec as P

CW = 8
CN = 128
ROWS = CW + 2
COLS = CN + 2
MESH = pl.DeviceIdType.MESH
GROUP = 4
PAIR = 2 * GROUP
EARLY = 11


def kernel(
    devices,
    scal_hbm,
    mass_hbm,
    freq_hbm,
    cell_hbm,
    owner_hbm,
    mixed_hbm,
    mean_hbm,
    out_a,
    out_b,
    got_a,
    got_b,
    near_a,
    near_b,
    ret_a,
    ret_b,
    scal_ref,
    freq_ref,
    cell_ref,
    owner_ref,
    left_even,
    left_odd,
    hot_ref,
    acc_a,
    acc_b,
    tile_a,
    tile_b,
    side_a,
    side_b,
    up_a,
    up_b,
    side_got_a,
    side_got_b,
    diag_a,
    diag_b,
    mean_a,
    mean_b,
    inverse_ref,
    idx_vm,
    idx_sm,
    row_buf,
    weight_ref,
    mixed_ref,
    mean_ref,
    store_sem,
    load_sem,
    hello_sem,
    idx_sem,
    send_sem,
    recv_sem,
    back_send,
    back_recv,
    halo_send,
    halo_recv,
):
    f32, bf16 = jnp.float32, jnp.bfloat16
    wide = lax.axis_index("wide")
    narrow = lax.axis_index("narrow")
    me = wide * 8 + narrow
    here = (lax.div(wide, 4), lax.rem(wide, 4), lax.div(narrow, 2), lax.rem(narrow, 2))

    def at_offset(offset, sign=1):
        z, x, y, c = (
            lax.rem(h + (d if sign > 0 else n - d), n) for h, d, n in zip(here, offset, (4, 4, 4, 2))
        )
        return z * 4 + x, y * 2 + c

    near_by = [(0, 0, 0, 1)]
    for d in (1, 3, 2):
        near_by += [(d, 0, 0, 0), (0, d, 0, 0), (0, 0, d, 0)]

    def two_axes(i):
        a, b = 1 + lax.div(i, 3), 1 + lax.rem(i, 3)
        on = [1 - lax.div(lax.rem(b - 1 + n, 3) + 1, 2) for n in (0, 2, 1)]
        return [(a, b, 0, 0), (b, 0, a, 0), (0, a, b, 0), (on[0] * a, on[1] * a, on[2] * a, 1)]

    def three_axes(i):
        a, b = 1 + lax.div(i, 3), 1 + lax.rem(i, 3)
        last = [(a, b, n, 0) for n in (1, 2, 3)]
        return [last[0], (a, b, 0, 1), last[1], (b, 0, a, 1), last[2], (0, a, b, 1)]

    def four_axes(i):
        a = 1 + i
        return [(a, b, 1 + (b + n) % 3, 1) for n in range(3) for b in (1, 2, 3)]

    classes = [(11, 9, two_axes), (47, 9, three_axes), (101, 3, four_axes)]

    def hello(sem):
        for offset in near_by:
            pl.semaphore_signal(sem, inc=1, device_id=at_offset(offset), device_id_type=MESH)

    barrier = pltpu.get_barrier_semaphore()
    hello(barrier)
    loads = [
        pltpu.make_async_copy(src, dst, load_sem.at[n])
        for n, (src, dst) in enumerate(
            (
                (owner_hbm, owner_ref),
                (scal_hbm, scal_ref),
                (mass_hbm, weight_ref.at[pl.ds(0, mass_hbm.shape[0])]),
                (cell_hbm, cell_ref),
                (freq_hbm, freq_ref),
            )
        )
    ]
    for copy in loads:
        copy.start()

    lanes = owner_ref.shape[1]
    weight_ref[lanes : lanes + 8, :] = jnp.zeros((8, CN), f32)
    acc_a[...] = jnp.zeros_like(acc_a)
    acc_b[...] = jnp.zeros_like(acc_b)
    loads[0].wait()
    along = jnp.broadcast_to(owner_ref[...], (lanes, lanes))
    down = along.T
    sub = lax.broadcasted_iota(jnp.int32, (lanes, lanes), 0)
    lane = lax.broadcasted_iota(jnp.int32, (lanes, lanes), 1)
    match = down == lane
    first = jnp.min(jnp.where(match, sub, lanes), axis=0, keepdims=True)
    second = jnp.max(jnp.where(match, sub, -1), axis=0, keepdims=True)
    earlier = jnp.where((down == along) & (sub < lane), 1, 0)
    place = 2 * owner_ref[...] + jnp.max(earlier, axis=0, keepdims=True)
    idx_vm[0:1, :] = jnp.minimum(first, lanes - 1)
    idx_vm[1:2, :] = jnp.maximum(second, 0)
    idx_vm[2:3, :] = first
    idx_vm[3:4, :] = jnp.where(second > first, second, lanes)
    idx_vm[4:5, :] = place
    idx_vm[5:8, :] = jnp.zeros((3, lanes), jnp.int32)
    to_scalar = pltpu.make_async_copy(idx_vm, idx_sm, idx_sem)
    to_scalar.start()
    to_scalar.wait()
    for copy in loads[1:]:
        copy.wait()

    outs, gots = (out_a, out_b), (got_a, got_b)
    nears, rets = (near_a, near_b), (ret_a, ret_b)
    accs, tiles, means = (acc_a, acc_b), (tile_a, tile_b), (mean_a, mean_b)

    def pack(half, dest, owner):
        for slot in range(2):
            b = idx_sm[slot, owner]
            m = weight_ref[pl.ds(idx_sm[2 + slot, owner], 1), :]
            dest[8 * slot : 8 * slot + 8, :] = scal_ref[b, 8 * half : 8 * half + 8, :] * m
            if half == 0:
                dest[16 + slot : 17 + slot, :] = m
                dest[18 + slot : 19 + slot, :] = cell_ref[pl.ds(b, 1), :].astype(f32)

    def send_to(half, p, offset):
        w, v = at_offset(offset)
        pack(half, outs[half].at[p], w * 8 + v)
        pltpu.make_async_remote_copy(
            outs[half].at[p],
            gots[half].at[p],
            send_sem.at[half],
            recv_sem.at[half, lax.div(p, PAIR)],
            device_id=(w, v),
            device_id_type=MESH,
        ).start()

    def send_class(half, base, steps, offsets):
        def body(i, carry):
            listed = offsets(i)
            for n, offset in enumerate(listed):
                send_to(half, base + len(listed) * i + n, offset)
            return carry

        lax.fori_loop(0, steps, body, 0)

    pl.semaphore_wait(barrier, len(near_by))
    hello(hello_sem.at[0])
    for n, offset in enumerate(near_by):
        send_to(0, 1 + n, offset)
    pl.semaphore_wait(hello_sem.at[0], len(near_by))
    hello(hello_sem.at[1])
    send_class(0, *classes[0])
    pl.semaphore_wait(hello_sem.at[1], len(near_by))
    hello(hello_sem.at[2])
    send_class(0, *classes[1])
    pl.semaphore_wait(hello_sem.at[2], len(near_by))
    send_class(0, *classes[2])
    pack(0, got_a.at[0], me)
    pack(1, got_b.at[0], me)
    for n, offset in enumerate(near_by):
        send_to(1, 1 + n, offset)
    for arguments in classes:
        send_class(1, *arguments)

    tile_row = lax.broadcasted_iota(jnp.int32, (16, CN), 0).astype(f32)
    row16 = tile_row.astype(bf16)
    none, one = jnp.zeros((16, CN), bf16), jnp.ones((16, CN), bf16)

    def place_of(cells):
        i = jnp.floor((cells + 0.5) * (1.0 / COLS))
        j = cells - i * COLS - 1.0
        return i, jnp.where(j < 0.0, COLS - 1.0, j)

    def fill_hot(p, slot, j):
        j16 = jnp.broadcast_to(j, (16, CN)).astype(bf16)
        for t in range(-(-COLS // 16)):
            hot_ref[p, 16 * t : 16 * t + 16, CN * slot : CN * slot + CN] = jnp.where(
                row16 + jnp.full((16, CN), 16 * t, bf16) == j16, one, none
            )

    def two_terms(value):
        high = value.astype(bf16).astype(f32)
        return jnp.concatenate([high, value - high], axis=0).astype(bf16)

    def build(half, p0, left_buf):
        for n in range(GROUP):
            for slot in range(2):
                at = (2 * n + slot) * CN
                p = p0 + n
                i, j = place_of(got_a[p, 18 + slot : 19 + slot, :])
                if half == 0:
                    fill_hot(p, slot, j)
                terms = two_terms(gots[half][p, 8 * slot : 8 * slot + 8, :])
                i16 = jnp.broadcast_to(i, (16, CN)).astype(bf16)
                for r in range(ROWS):
                    left_buf[16 * r : 16 * r + 16, at : at + CN] = jnp.where(
                        i16 == jnp.full((16, CN), r, bf16), terms, none
                    )
                if half == 0:
                    m16 = jnp.broadcast_to(got_a[p, 16 + slot : 17 + slot, :], (16, CN))
                    mhi = m16.astype(bf16)
                    mlo = (m16 - mhi.astype(f32)).astype(bf16)
                    mask = i16 == row16
                    left_buf[160:176, at : at + CN] = jnp.where(mask, mhi, none)
                    left_buf[176:192, at : at + CN] = jnp.where(mask, mlo, none)

    def add_up(half, p0, left_buf):
        rows = accs[half].shape[0]
        for n in range(GROUP):
            accs[half][:, 0:144] += lax.dot_general(
                left_buf[0:rows, 256 * n : 256 * n + 256],
                hot_ref[p0 + n],
                (((1,), (1,)), ((), ())),
                preferred_element_type=f32,
            )

    def deposit(half, t, first=0):
        p = t * PAIR
        span = pl.ds(p + first, PAIR - first)
        pltpu.make_async_copy(
            outs[half].at[span], gots[half].at[span], recv_sem.at[half, t]
        ).wait()
        build(half, p, left_even)
        build(half, p + GROUP, left_odd)
        add_up(half, p, left_even)
        add_up(half, p + GROUP, left_odd)

    def deposit_range(half, low, high):
        def body(t, carry):
            deposit(half, t)
            return carry

        lax.fori_loop(low, high, body, 0)

    above, below = (wide + 15) % 16, (wide + 1) % 16
    before, after = (narrow + 7) % 8, (narrow + 1) % 8
    at_lanes = [
        lax.broadcasted_iota(jnp.int32, (tile.shape[0], 128), 1) for tile in tiles
    ]

    def halo_copies(half):
        tile_ref, side_buf = tiles[half], (side_a, side_b)[half]
        up, side_got, diag = ((up_a, side_got_a, diag_a), (up_b, side_got_b, diag_b))[half]
        rows, edge = tile_ref.shape[0], up.shape[1]
        top, bottom = pl.ds(0, edge), pl.ds(rows - edge, edge)
        listed = [
            (tile_ref.at[top], up.at[1], (above, narrow)),
            (tile_ref.at[bottom], up.at[0], (below, narrow)),
            (side_buf.at[0], side_got.at[1], (wide, before)),
            (side_buf.at[1], side_got.at[0], (wide, after)),
            (side_buf.at[0, top], diag.at[3], (above, before)),
            (side_buf.at[0, bottom], diag.at[1], (below, before)),
            (side_buf.at[1, top], diag.at[2], (above, after)),
            (side_buf.at[1, bottom], diag.at[0], (below, after)),
        ]
        return [
            pltpu.make_async_remote_copy(
                src,
                dst,
                halo_send.at[half, n],
                halo_recv.at[half, n],
                device_id=to,
                device_id_type=MESH,
            )
            for n, (src, dst, to) in enumerate(listed)
        ]

    def halo_start(half):
        acc, tile_ref, side_buf = accs[half], tiles[half], (side_a, side_b)[half]
        start = 8 if half == 0 else 0
        for r in range(ROWS):
            tile_ref[start + 8 * r : start + 8 * r + 8, :] = (
                acc[16 * r : 16 * r + 8, :] + acc[16 * r + 8 : 16 * r + 16, :]
            )
        if half == 0:
            tile_ref[0:8, :] = acc[160:168, :] + acc[176:184, :]
            tile_ref[88:96, :] = acc[168:176, :] + acc[184:192, :]
        own, rest = tile_ref[:, 0:128], tile_ref[:, 128:256]
        at_lane = at_lanes[half]
        side_buf[0] = jnp.where(at_lane == 127, pltpu.roll(rest, 126, 1), own)
        side_buf[1] = jnp.where(at_lane == 0, rest, pltpu.roll(own, 2, 1))
        for copy in halo_copies(half):
            copy.start()

    def halo_finish(half):
        for copy in halo_copies(half):
            copy.wait()
        tile_ref, at_lane = tiles[half], at_lanes[half]
        up, side_got, diag = ((up_a, side_got_a, diag_a), (up_b, side_got_b, diag_b))[half]

        def unfold(high, low):
            middle = jnp.zeros((48, high.shape[1]), f32)
            if half == 0:
                parts = [high[16:24], high[0:16], middle, low[8:24], low[0:8]]
            else:
                parts = [high, middle, low]
            return jnp.concatenate(parts, axis=0)

        from_left = side_got[0] + unfold(diag[0], diag[2])
        from_right = side_got[1] + unfold(diag[1], diag[3])
        vertical = unfold(up[0], up[1])
        own = (
            tile_ref[:, 0:128]
            + vertical[:, 0:128]
            + jnp.where(at_lane == 0, from_left, 0.0)
            + jnp.where(at_lane == 127, from_right, 0.0)
        )
        rest = (
            tile_ref[:, 128:256]
            + vertical[:, 128:256]
            + jnp.where(at_lane == 1, from_left, 0.0)
            + jnp.where(at_lane == 0, from_right, 0.0)
        )
        total = jnp.concatenate([own, rest], axis=1)
        if half == 0:
            inverse_ref[0:8, :] = 1.0 / (total[0:8, :] + 1.0)
            inverse_ref[8:16, :] = 1.0 / (total[88:96, :] + 1.0)
        start = 8 if half == 0 else 0
        for r in range(ROWS):
            mean = total[start + 8 * r : start + 8 * r + 8, :] * inverse_ref[r : r + 1, :]
            if 1 <= r <= CW:
                mean_ref[8 * half : 8 * half + 8, r - 1, :] = mean[:, 0:CN]
            means[half][16 * r : 16 * r + 16, :] = two_terms(mean)

    def lookup(half, p, count):
        for n in range(count):
            found = jnp.dot(
                means[half][:, 0:144], hot_ref[p + n], preferred_element_type=f32
            )
            for slot in range(2):
                i, _ = place_of(got_a[p + n, 18 + slot : 19 + slot, :])
                i16 = jnp.broadcast_to(i, (16, CN))
                cut = slice(CN * slot, CN * slot + CN)
                near = found[0:16, cut]
                for r in range(1, ROWS):
                    near = jnp.where(i16 == float(r), found[16 * r : 16 * r + 16, cut], near)
                nears[half][2 * (p + n) + slot] = near[0:8] + near[8:16]

    def give_back(half, p, offset):
        pltpu.make_async_remote_copy(
            nears[half].at[pl.ds(2 * p, 2)],
            rets[half].at[pl.ds(2 * me, 2)],
            back_send.at[half],
            back_recv.at[half],
            device_id=at_offset(offset, -1),
            device_id_type=MESH,
        ).start()

    def return_class(half, base, steps, offsets):
        def body(i, carry):
            listed = offsets(i)
            p = base + len(listed) * i
            lookup(half, p, len(listed))
            for n, offset in enumerate(listed):
                give_back(half, p + n, offset)
            return carry

        lax.fori_loop(0, steps, body, 0)

    def return_near(half):
        for p in (8, 4, 0):
            lookup(half, p, min(4, 11 - p))
            for n in range(p, min(p + 4, 11)):
                if n:
                    give_back(half, n, near_by[n - 1])
        rets[half][pl.ds(2 * me, 2)] = nears[half][0:2]

    pairs = devices // PAIR
    deposit(0, 0, 1)
    deposit_range(0, 1, pairs)
    halo_start(0)
    deposit(1, 0, 1)
    deposit_range(1, 1, EARLY)
    halo_finish(0)
    return_class(0, *classes[2])
    return_class(0, *classes[1])
    deposit_range(1, EARLY, pairs)
    halo_start(1)
    return_class(0, *classes[0])
    return_near(0)
    halo_finish(1)
    stores = [pltpu.make_async_copy(mean_ref, mean_hbm, store_sem.at[2])]
    stores[0].start()
    for arguments in reversed(classes):
        return_class(1, *arguments)
    return_near(1)

    others = pl.ds(2, 2 * (devices - 1))

    def returned(half):
        pltpu.make_async_copy(
            nears[half].at[others], rets[half].at[others], back_recv.at[half]
        ).wait()

    returned(0)

    def read_rate(b, carry):
        row_buf[pl.ds(b, 1), :] = ret_a[idx_sm[4, b], 0:1, :]
        return carry

    lax.fori_loop(0, lanes, read_rate, 0, unroll=8)
    row_buf[...] = jnp.exp(-freq_ref[...] * (1.5 + jnp.tanh(row_buf[...])))

    def mix(half):
        def body(b, carry):
            near = rets[half][idx_sm[4, b]]
            own = scal_ref[b, 8 * half : 8 * half + 8, :]
            mixed_ref[b, 8 * half : 8 * half + 8, :] = near + (own - near) * row_buf[pl.ds(b, 1), :]
            return carry

        lax.fori_loop(0, lanes, body, 0, unroll=8)

    def store(half):
        rows = pl.ds(8 * half, 8)
        copy = pltpu.make_async_copy(
            mixed_ref.at[:, rows], mixed_hbm.at[:, rows], store_sem.at[half]
        )
        copy.start()
        stores.append(copy)

    mix(0)
    store(0)
    returned(1)
    mix(1)
    store(1)

    for half in range(2):
        rest_of = pl.ds(1, devices - 1)
        pltpu.make_async_copy(
            outs[half].at[rest_of], gots[half].at[rest_of], send_sem.at[half]
        ).wait()
        pltpu.make_async_copy(
            nears[half].at[others], rets[half].at[others], back_send.at[half]
        ).wait()
    for copy in stores:
        copy.wait()


def per_device(scalars, mass, frequency, cell, owner):
    devices = lax.axis_size("wide") * lax.axis_size("narrow")
    blocks, count, per_block = scalars.shape
    f32, bf16 = jnp.float32, jnp.bfloat16
    hbm = pl.BlockSpec(memory_space=pltpu.HBM)
    return pl.pallas_call(
        functools.partial(kernel, devices),
        out_shape=(
            jax.ShapeDtypeStruct((blocks, count, per_block), f32),
            jax.ShapeDtypeStruct((count, CW, CN), f32),
        ),
        in_specs=[hbm] * 5,
        out_specs=(hbm, hbm),
        scratch_shapes=[
            pltpu.VMEM((devices, 20, per_block), f32),
            pltpu.VMEM((devices, 16, per_block), f32),
            pltpu.VMEM((devices, 20, per_block), f32),
            pltpu.VMEM((devices, 16, per_block), f32),
            *[pltpu.VMEM((2 * devices, 8, per_block), f32)] * 4,
            pltpu.VMEM((blocks, count, per_block), f32),
            pltpu.VMEM((blocks, per_block), f32),
            pltpu.VMEM((blocks, per_block), jnp.int32),
            pltpu.VMEM((1, blocks), jnp.int32),
            pltpu.VMEM((192, GROUP * 256), bf16),
            pltpu.VMEM((192, GROUP * 256), bf16),
            pltpu.VMEM((devices, 144, 256), bf16),
            pltpu.VMEM((192, 256), f32),
            pltpu.VMEM((160, 256), f32),
            pltpu.VMEM((96, 256), f32),
            pltpu.VMEM((80, 256), f32),
            pltpu.VMEM((2, 96, 128), f32),
            pltpu.VMEM((2, 80, 128), f32),
            pltpu.VMEM((2, 24, 256), f32),
            pltpu.VMEM((2, 16, 256), f32),
            pltpu.VMEM((2, 96, 128), f32),
            pltpu.VMEM((2, 80, 128), f32),
            pltpu.VMEM((4, 24, 128), f32),
            pltpu.VMEM((4, 16, 128), f32),
            pltpu.VMEM((160, 256), bf16),
            pltpu.VMEM((160, 256), bf16),
            pltpu.VMEM((16, 256), f32),
            pltpu.VMEM((8, blocks), jnp.int32),
            pltpu.SMEM((8, blocks), jnp.int32),
            pltpu.VMEM((blocks, per_block), f32),
            pltpu.VMEM((blocks + 8, per_block), f32),
            pltpu.VMEM((blocks, count, per_block), f32),
            pltpu.VMEM((count, CW, CN), f32),
            pltpu.SemaphoreType.DMA((3,)),
            pltpu.SemaphoreType.DMA((5,)),
            pltpu.SemaphoreType.REGULAR((3,)),
            pltpu.SemaphoreType.DMA,
            pltpu.SemaphoreType.DMA((2,)),
            pltpu.SemaphoreType.DMA((2, devices // PAIR)),
            pltpu.SemaphoreType.DMA((2,)),
            pltpu.SemaphoreType.DMA((2,)),
            pltpu.SemaphoreType.DMA((2, 8)),
            pltpu.SemaphoreType.DMA((2, 8)),
        ],
        compiler_params=pltpu.CompilerParams(
            collective_id=0, has_side_effects=True, vmem_limit_bytes=64 << 20
        ),
        name="mixing",
    )(scalars, mass, frequency, cell, owner.reshape(1, blocks))


def solution(mesh):
    held = P(("wide", "narrow"), None)
    block = P(("wide", "narrow"), None, None)
    return jax.shard_map(
        per_device,
        mesh=mesh,
        in_specs=(block, held, held, held, held),
        out_specs=(block, P(None, "wide", "narrow")),
        check_vma=False,
    )
```
